256 devices in a mesh: gx: 16 (over z, core), gy: 16 (over x, y).
Axes of the slice: x: 4, y: 4, z: 8, core: 2. Of those that a mesh axis runs over, the one named last changes fastest.
Arguments:
- instruments: bfloat16 [64, 2048, 4096], P(None, 'gx', 'gy'), may hold values from -40 to 40
- regressors: bfloat16 [64, 2048, 4096], P(None, 'gx', 'gy'), may hold values from -6 to 6
- outcome: float32 [2048, 4096], P('gx', 'gy'), may hold values from -6 to 6
- land_mask: int32 [2048, 4096], P('gx', 'gy'), may hold values from 0 to 1, as said below
- coefficients: float32 [64], replicated, may hold values from -4 to 4
- weighting: float32 [64, 64], replicated, may hold values from -1 to 2, as said below
Outputs:
- smoothed: bfloat16 [64, 2048, 4096], P(None, 'gx', 'gy')
- hac_cov: float32 [64, 64], replicated
- new_coefficients: float32 [64], replicated
The draws below stay inside these ranges and needn't reach their ends.
Inputs may be any that keep to these rules, and one draw needn't show every extreme that they name: `land_mask`: 1 marks land, 0 water. `weighting`: symmetric positive definite.
All inputs are finite; a program needn't handle non-finite values.
Results may differ from the reference program's by a relative error of at most 0.0012.
The reference program's roundings to bfloat16 on the way (of `half_coefficients`, `moments` and `row_smoothed`) count: a program that leaves them out, or rounds other values in their place, can miss the bound.
Values may be sent and summed in bfloat16 or wider, within the bound.
A program may use at most 128 MiB of HBM per device.

```python
import jax
import jax.numpy as jnp
from jax import lax

K = 64
P_SIZE = 64
B = 64
CX = 128
NX = 2048
NY = 4096


def shared_parts(key):
    first_key = jax.random.fold_in(key, 0)
    normal_part = jax.random.truncated_normal(first_key, -4.0, 4.0, (K, NX, NY), jnp.float32)
    return normal_part


def draw_instruments(key, part):
    normal_part = shared_parts(key)
    key = jax.random.fold_in(key, 1)
    scales = jnp.exp(jax.random.uniform(key, (K, 1, 1), jnp.float32, jnp.log(0.3), jnp.log(3.0)))
    spatial_ramp = 1.0 + 2.0 * jnp.arange(NX, dtype=jnp.float32).reshape(1, NX, 1) / max(NX - 1, 1)
    common_part = normal_part
    return (common_part * scales * spatial_ramp).astype(jnp.bfloat16)


def draw_regressors(key, part):
    normal_part = shared_parts(key)
    key = jax.random.fold_in(key, 2)
    idiosyncratic = jax.random.truncated_normal(key, -4.0, 4.0, (P_SIZE, NX, NY), jnp.float32)
    common_part = normal_part
    return (0.6 * common_part + 0.8 * idiosyncratic).astype(jnp.bfloat16)


def draw_land_mask(key, part):
    key = jax.random.fold_in(key, 3)
    scores = jax.random.randint(key, (NX, NY), 0, 1000, jnp.int32)
    row_ids = lax.broadcasted_iota(jnp.int32, (NX, NY), 0)
    threshold = 300 + 600 * row_ids // max(NX - 1, 1)
    return (scores < threshold).astype(jnp.int32)


def draw_weighting(key, part):
    key = jax.random.fold_in(key, 4)
    diag_key, side_key = jax.random.split(key)
    diagonal = jnp.exp(jax.random.uniform(diag_key, (K,), jnp.float32, 0.0, jnp.log(2.0)))
    half_width = 0.9 / K
    off_diagonal = jax.random.uniform(side_key, (K, K), jnp.float32, -half_width, half_width)
    symmetric = 0.5 * (off_diagonal + off_diagonal.T)
    identity = jnp.eye(K, dtype=jnp.float32)
    return symmetric * (1.0 - identity) + identity * diagonal[None, :]


def block_levels(own_key, extent, cuts, least, top_value):
    gain, own = 1.0, jax.random.fold_in(own_key, 6)
    for position, shards_of in cuts:
        heights = jnp.exp(jax.random.uniform(jax.random.fold_in(own, position), (shards_of,), jnp.float32, least / len(cuts), top_value / len(cuts)))
        gain = gain * jnp.repeat(heights, extent[position] // shards_of).reshape([-1 if axis == position else 1 for axis in range(len(extent))])
    return gain


def gaussian(rng, dims, deviation, limit, cuts=(), kind=jnp.bfloat16):
    array = deviation * jax.random.normal(rng, dims, jnp.float32)
    if cuts:
        array = array * block_levels(rng, dims, cuts, -0.22, 0.18)
    return jnp.clip(array, -limit, limit).astype(kind)


def setup_inputs(seed: int = 0) -> dict:
    streams_of = jax.random.split(jax.random.key(seed), 7)
    return {
        "instruments": draw_instruments(jax.random.fold_in(streams_of[6], 71), 0),
        "regressors": draw_regressors(jax.random.fold_in(streams_of[6], 71), 0),
        "outcome": gaussian(streams_of[2], (NX, NY), 1.0, 6.0, ((0, 16), (1, 16)), jnp.float32),
        "land_mask": draw_land_mask(jax.random.fold_in(streams_of[6], 71), 0),
        "coefficients": gaussian(streams_of[4], (P_SIZE,), 1.0, 4.0, (), jnp.float32),
        "weighting": draw_weighting(jax.random.fold_in(streams_of[6], 71), 0),
    }


step_rate = 0.05


def bartlett_taps():
    offsets = jnp.arange(-B, B + 1)
    return (B + 1 - jnp.abs(offsets)).astype(jnp.float32)


def smooth_along(values_in, direction):
    kernel = bartlett_taps()
    if direction == 1:
        kernel = kernel.reshape(1, 1, 1, -1)
        padding = [(0, 0), (B, B)]
    else:
        kernel = kernel.reshape(1, 1, -1, 1)
        padding = [(B, B), (0, 0)]
    result = lax.conv_general_dilated(values_in[None, None], kernel, (1, 1), padding, precision=lax.Precision.HIGHEST)
    return result[0, 0]


def reference(instruments, regressors, outcome, land_mask, coefficients, weighting):
    half_coefficients = coefficients.astype(jnp.bfloat16)
    fitted = lax.dot_general(half_coefficients.reshape(1, -1), regressors.reshape(P_SIZE, NX * NY), (((1,), (0,)), ((), ())), preferred_element_type=jnp.float32).reshape(NX, NY)
    land_float = land_mask.astype(jnp.float32)
    weighted = land_float * (outcome - fitted)

    def per_channel(channel_in):
        moment_map = (channel_in.astype(jnp.float32) * weighted).astype(jnp.bfloat16)
        moment_map = lax.optimization_barrier(moment_map)
        row_smoothed = (smooth_along(moment_map.astype(jnp.float32), 1) * (1.0 / (B + 1))).astype(jnp.bfloat16)
        row_smoothed = lax.optimization_barrier(row_smoothed)
        smooth_map = (smooth_along(row_smoothed.astype(jnp.float32), 0) * (1.0 / (B + 1) ** 2)).astype(jnp.bfloat16)
        return moment_map, smooth_map, jnp.sum(moment_map.astype(jnp.float32))

    moments, smoothed, moment_sums = lax.map(per_channel, instruments)

    def per_block(block_index, running):
        cov_sum, jac_sum = running
        first_row = (block_index * CX).astype(jnp.int32)
        moment_block = lax.dynamic_slice_in_dim(moments, first_row, CX, 1).reshape(K, -1).astype(jnp.float32)
        smooth_block = lax.dynamic_slice_in_dim(smoothed, first_row, CX, 1).reshape(K, -1).astype(jnp.float32)
        inst_block = lax.dynamic_slice_in_dim(instruments, first_row, CX, 1).reshape(K, -1).astype(jnp.float32)
        land_block = lax.dynamic_slice_in_dim(land_float, first_row, CX, 0)
        reg_block = (lax.dynamic_slice_in_dim(regressors, first_row, CX, 1).astype(jnp.float32) * land_block[None]).reshape(P_SIZE, -1)
        cov_sum = cov_sum + jnp.dot(moment_block, smooth_block.T, precision=lax.Precision.HIGHEST)
        jac_sum = jac_sum + jnp.dot(inst_block, reg_block.T, precision=lax.Precision.HIGHEST)
        return cov_sum, jac_sum

    start_sums = (jnp.zeros((K, K), jnp.float32), jnp.zeros((K, P_SIZE), jnp.float32))
    cov_sum, jac_sum = lax.fori_loop(0, NX // CX, per_block, start_sums)
    land_total = jnp.sum(land_float)
    hac_cov = cov_sum * ((B + 1) / land_total)
    mean_moment = moment_sums / land_total
    jacobian = -jac_sum / land_total
    gradient = 2.0 * jnp.dot(jacobian.T, jnp.dot(weighting, mean_moment, precision=lax.Precision.HIGHEST), precision=lax.Precision.HIGHEST)
    new_coefficients = coefficients - step_rate * gradient
    return smoothed, hac_cov, new_coefficients
```

```python
import functools

import jax
import jax.numpy as jnp
from jax import lax
from jax.experimental import pallas as pl
from jax.experimental.pallas import tpu as pltpu
from jax.sharding import PartitionSpec as P

B = 64
step_rate = 0.05
MESH = pl.DeviceIdType.MESH
F32 = jnp.float32
BF16 = jnp.bfloat16
CH = 8
GROUP = 16
SUB = 16


def iota(shape, dim):
    return lax.broadcasted_iota(jnp.int32, shape, dim)


def dot(a, b):
    return lax.dot_general(a, b, (((1,), (0,)), ((), ())), preferred_element_type=F32)


def dot_t(a, b):
    return lax.dot_general(a, b, (((1,), (1,)), ((), ())), preferred_element_type=F32)


def hat(distance):
    return jnp.maximum(B + 1 - jnp.abs(distance), 0).astype(F32).astype(BF16)


def kernel(
    nx,
    ny,
    inst_h,
    reg_h,
    outcome_h,
    land_h,
    coef_s,
    coef_v,
    wgt_v,
    s_h,
    hac_v,
    new_v,
    inst,
    reg,
    outcome,
    land,
    coefs,
    weighted,
    land_half,
    mom,
    send_l,
    send_r,
    y_l,
    y_r,
    rows_sm,
    sm,
    w_top,
    w_bot,
    w_col,
    acc,
    cov,
    jac,
    sums,
    part,
    got1,
    sum1,
    got2,
    sum2,
    got3,
    in_sem,
    reg_sem,
    inst_sem,
    yl_send,
    yl_recv,
    yr_send,
    yr_recv,
    zt_send,
    zt_recv,
    zb_send,
    zb_recv,
    out_sem,
    ar_send,
    ar_recv,
):
    gx = lax.axis_index("gx")
    gy = lax.axis_index("gy")
    channels, rows, cols = inst.shape
    half = rows // 2
    n_chunks = channels // CH
    n_groups = channels // GROUP
    n_sub = rows // SUB
    reg_rows = rows // 4

    def outcome_copy():
        return pltpu.make_async_copy(outcome_h, outcome, in_sem.at[0])

    def land_copy():
        return pltpu.make_async_copy(land_h, land, in_sem.at[1])

    def reg_copy(r):
        at = pl.ds(pl.multiple_of(r * reg_rows, reg_rows), reg_rows)
        return pltpu.make_async_copy(reg_h.at[:, at, :], reg.at[:, at, :], reg_sem.at[r])

    def inst_copy(g):
        at = pl.ds(g * GROUP, GROUP)
        return pltpu.make_async_copy(inst_h.at[at], inst.at[at], inst_sem.at[g])

    outcome_copy().start()
    land_copy().start()
    for r in range(4):
        reg_copy(r).start()
    for g in range(n_groups):
        inst_copy(g).start()

    barrier = pltpu.get_barrier_semaphore()

    def greet_x(g, carry):
        @pl.when(g != gx)
        def _():
            pl.semaphore_signal(barrier, inc=1, device_id=(g, gy), device_id_type=MESH)

        return carry

    def greet_y(g, carry):
        @pl.when(g != gy)
        def _():
            pl.semaphore_signal(barrier, inc=1, device_id=(gx, g), device_id_type=MESH)

        return carry

    lax.fori_loop(0, nx, greet_x, 0)
    lax.fori_loop(0, ny, greet_y, 0)

    for p in range(channels):
        coefs[p : p + 1, :] = jnp.full((1, cols), coef_s[p], F32)
    coefs[...] = coefs[...].astype(BF16).astype(F32)

    src = iota((cols, cols), 0)
    dst = iota((cols, cols), 1)
    own = hat(src - dst)
    w_top[0:cols, :] = own
    w_bot[0:cols, :] = own
    low = src % half
    side = jnp.where(src < 2 * half, low - half, low + cols)
    ramp = jnp.maximum(B + 1 - jnp.abs(side - dst), 0).astype(F32)
    is_top = (src // half) % 2 == 0
    w_top[cols : 2 * cols, :] = jnp.where(is_top, ramp, 0.0).astype(BF16)
    w_bot[cols : 2 * cols, :] = jnp.where(is_top, 0.0, ramp).astype(BF16)
    w_col[...] = hat(iota((rows, 2 * rows), 1) - half - iota((rows, 2 * rows), 0))

    @pl.when(gy == 0)
    def _():
        y_l[...] = jnp.zeros_like(y_l)

    @pl.when(gy == ny - 1)
    def _():
        y_r[...] = jnp.zeros_like(y_r)

    def clear(start):
        def body(k, carry):
            rows_sm[k, start : start + half, :] = jnp.zeros((half, cols), BF16)
            return carry

        lax.fori_loop(0, channels, body, 0)

    @pl.when(gx == 0)
    def _():
        clear(0)

    @pl.when(gx == nx - 1)
    def _():
        clear(rows + half)

    outcome_copy().wait()
    land_copy().wait()

    def residuals(r, carry):
        reg_copy(r).wait()
        at = pl.ds(pl.multiple_of(r * reg_rows, reg_rows), reg_rows)

        def add(q, total):
            for u in range(8):
                p = q * 8 + u
                total = total + reg[p, at, :].astype(F32) * coefs[pl.ds(p, 1), :]
            return total

        fitted = lax.fori_loop(0, channels // 8, add, jnp.zeros((reg_rows, cols), F32))
        land_float = land[at, :].astype(F32)
        weighted[at, :] = land_float * (outcome[at, :] - fitted)
        land_half[at, :] = land_float.astype(BF16)
        return carry

    lax.fori_loop(0, 4, residuals, 0)

    pl.semaphore_wait(barrier, nx - 1 + ny - 1)

    def to_left(c):
        at = pl.ds(c * CH, CH)
        return pltpu.make_async_remote_copy(
            src_ref=send_l.at[at],
            dst_ref=y_r.at[at],
            send_sem=yl_send.at[c],
            recv_sem=yr_recv.at[c],
            device_id=(gx, gy - 1),
            device_id_type=MESH,
        )

    def to_right(c):
        at = pl.ds(c * CH, CH)
        return pltpu.make_async_remote_copy(
            src_ref=send_r.at[at],
            dst_ref=y_l.at[at],
            send_sem=yr_send.at[c],
            recv_sem=yl_recv.at[c],
            device_id=(gx, gy + 1),
            device_id_type=MESH,
        )

    def to_upper(c):
        at = pl.ds(c * CH, CH)
        return pltpu.make_async_remote_copy(
            src_ref=rows_sm.at[at, half : 2 * half, :],
            dst_ref=rows_sm.at[at, 3 * half : 4 * half, :],
            send_sem=zt_send.at[c],
            recv_sem=zb_recv.at[c],
            device_id=(gx - 1, gy),
            device_id_type=MESH,
        )

    def to_lower(c):
        at = pl.ds(c * CH, CH)
        return pltpu.make_async_remote_copy(
            src_ref=rows_sm.at[at, 2 * half : 3 * half, :],
            dst_ref=rows_sm.at[at, 0:half, :],
            send_sem=zb_send.at[c],
            recv_sem=zt_recv.at[c],
            device_id=(gx + 1, gy),
            device_id_type=MESH,
        )

    has_left, has_right = gy > 0, gy < ny - 1
    has_upper, has_lower = gx > 0, gx < nx - 1

    first_lanes = iota((SUB, 128), 1) < B

    def moments(c, carry):
        @pl.when(c % (GROUP // CH) == 0)
        def _():
            inst_copy(c // (GROUP // CH)).wait()

        def channel(u, inner):
            k = c * CH + u
            for r in range(0, half, SUB):
                upper, lower = slice(r, r + SUB), slice(half + r, half + r + SUB)
                top = inst[k, upper, :].astype(F32) * weighted[upper, :]
                bot = inst[k, lower, :].astype(F32) * weighted[lower, :]
                mom[k, upper, :] = top.astype(BF16)
                mom[k, lower, :] = bot.astype(BF16)
                left = jnp.where(first_lanes, top[:, :128], pltpu.roll(bot[:, :128], B, 1))
                right = jnp.where(first_lanes, pltpu.roll(top[:, cols - 128 :], B, 1), bot[:, cols - 128 :])
                send_l[k, upper, :] = left.astype(BF16)
                send_r[k, upper, :] = right.astype(BF16)
            return inner

        lax.fori_loop(0, CH, channel, 0)

        @pl.when(has_left)
        def _():
            to_left(c).start()

        @pl.when(has_right)
        def _():
            to_right(c).start()

        return carry

    lax.fori_loop(0, n_chunks, moments, 0)

    lanes = iota((1, SUB, GROUP * SUB), 2)
    diagonal = lanes % SUB == iota((1, SUB, GROUP * SUB), 1)

    def fold(total, g):
        kept = jnp.where(diagonal, total.reshape(channels, SUB, GROUP * SUB), 0.0)
        kept = jnp.sum(kept, axis=1)
        pick = iota((GROUP * SUB, 128), 0) // SUB + g * GROUP == iota((GROUP * SUB, 128), 1)
        return lax.dot_general(
            kept,
            pick.astype(F32),
            (((1,), (0,)), ((), ())),
            precision=lax.Precision.HIGHEST,
            preferred_element_type=F32,
        )

    def block(ref, first, count, b):
        at = pl.ds(pl.multiple_of(b * SUB, SUB), SUB)
        return ref[pl.ds(first, count), at, :]

    def jac_group(g):
        acc[...] = jnp.zeros_like(acc)

        def step(b, carry):
            land_b = land_half[pl.ds(pl.multiple_of(b * SUB, SUB), SUB), :]
            lhs = (block(inst, 0, channels, b) * land_b[None]).reshape(channels * SUB, cols)
            rhs = block(reg, g * GROUP, GROUP, b).reshape(GROUP * SUB, cols)
            acc[...] += dot_t(lhs, rhs)
            return carry

        lax.fori_loop(0, n_sub, step, 0)
        jac[...] += fold(acc[...], g)

    def cov_group(g):
        acc[...] = jnp.zeros_like(acc)

        def step(b, carry):
            lhs = block(mom, 0, channels, b).reshape(channels * SUB, cols)
            rhs = block(sm, g * GROUP, GROUP, b).reshape(GROUP * SUB, cols)
            acc[...] += dot_t(lhs, rhs)
            return carry

        lax.fori_loop(0, n_sub, step, 0)
        cov[...] += fold(acc[...], g)

    def sum_group(g):
        for u in range(0, GROUP, 8):
            at = pl.ds(pl.multiple_of(g * GROUP + u, 8), 8)
            sums[at, :] = jnp.sum(mom[at].astype(F32), axis=1)

    cov[...] = jnp.zeros_like(cov)
    jac[...] = jnp.zeros_like(jac)

    def out_copy(c):
        at = pl.ds(c * CH, CH)
        return pltpu.make_async_copy(sm.at[at], s_h.at[at], out_sem.at[c])

    def smooth_rows(c):
        @pl.when(has_left)
        def _():
            to_right(c).wait_recv()

        @pl.when(has_right)
        def _():
            to_left(c).wait_recv()

        at = pl.ds(c * CH, CH)
        edges = jnp.concatenate(
            [y_l[at].reshape(CH * half, 128), y_r[at].reshape(CH * half, 128)], axis=1
        )
        for start, weights in ((0, w_top), (half, w_bot)):
            here = mom[at, start : start + half, :].reshape(CH * half, cols)
            total = dot(jnp.concatenate([here, edges], axis=1), weights[...])
            rows_sm[at, half + start : 2 * half + start, :] = (
                (total * (1.0 / (B + 1))).astype(BF16).reshape(CH, half, cols)
            )

        @pl.when(has_upper)
        def _():
            to_upper(c).start()

        @pl.when(has_lower)
        def _():
            to_lower(c).start()

    def smooth_columns(c):
        @pl.when(has_upper)
        def _():
            to_lower(c).wait_recv()

        @pl.when(has_lower)
        def _():
            to_upper(c).wait_recv()

        def channel(u, inner):
            k = c * CH + u
            total = dot(w_col[...], rows_sm[k])
            sm[k] = (total * (1.0 / (B + 1) ** 2)).astype(BF16)
            return inner

        lax.fori_loop(0, CH, channel, 0)
        out_copy(c).start()

    def pipeline(t, carry):
        @pl.when(t < n_chunks)
        def _():
            smooth_rows(t)

        @pl.when(t < n_groups)
        def _():
            jac_group(t)
            sum_group(t)

        @pl.when(t >= 1)
        def _():
            smooth_columns(t - 1)

        @pl.when(jnp.logical_and(t >= 1, t % (GROUP // CH) == 0))
        def _():
            cov_group(t // (GROUP // CH) - 1)

        return carry

    lax.fori_loop(0, n_chunks + 1, pipeline, 0)

    pieces = channels // 8
    own_pieces = 2 * pieces // nx
    count = jnp.sum(jnp.sum(land_half[...].astype(F32), axis=0, keepdims=True), axis=1, keepdims=True)
    columns = jnp.sum(sums[...], axis=1, keepdims=True)
    right_half = iota((channels, 128), 1) >= channels
    as_row = jnp.sum(
        jnp.where(iota((channels, 128), 1) - channels == iota((channels, 128), 0), columns, 0.0), axis=0, keepdims=True
    )
    part[0:pieces] = jnp.where(right_half, count, cov[...]).reshape(pieces, 8, 128)
    part[pieces : 2 * pieces] = jnp.where(right_half, as_row, jac[...]).reshape(pieces, 8, 128)

    def exchange(number, peers, me, copy, landed, sent):
        def send(g, carry):
            @pl.when(g != me)
            def _():
                copy(g).start()

            return carry

        lax.fori_loop(0, peers, send, 0)
        pltpu.make_async_copy(landed, landed, ar_recv.at[number]).wait()
        pltpu.make_async_copy(sent, sent, ar_send.at[number]).wait()

    def own(g):
        return pl.ds(g * own_pieces, own_pieces)

    def scatter(g):
        return pltpu.make_async_remote_copy(
            src_ref=part.at[own(g)],
            dst_ref=got1.at[gx],
            send_sem=ar_send.at[0],
            recv_sem=ar_recv.at[0],
            device_id=(g, gy),
            device_id_type=MESH,
        )

    def across(g):
        return pltpu.make_async_remote_copy(
            src_ref=sum1,
            dst_ref=got2.at[gy],
            send_sem=ar_send.at[1],
            recv_sem=ar_recv.at[1],
            device_id=(gx, g),
            device_id_type=MESH,
        )

    def gather(g):
        return pltpu.make_async_remote_copy(
            src_ref=sum2,
            dst_ref=got3.at[own(gx)],
            send_sem=ar_send.at[2],
            recv_sem=ar_recv.at[2],
            device_id=(g, gy),
            device_id_type=MESH,
        )

    got1[gx] = part[own(gx)]
    exchange(0, nx, gx, scatter, got1.at[0 : nx - 1], got1.at[0 : nx - 1])
    sum1[...] = jnp.sum(got1[...], axis=0)
    got2[gy] = sum1[...]
    exchange(1, ny, gy, across, got2.at[0 : ny - 1], got2.at[0 : ny - 1])
    sum2[...] = jnp.sum(got2[...], axis=0)
    got3[own(gx)] = sum2[...]
    rest = got3.at[0 : (nx - 1) * own_pieces]
    exchange(2, nx, gx, gather, rest, rest)

    first = got3[0:pieces].reshape(channels, 128)
    second = got3[pieces : 2 * pieces].reshape(channels, 128)
    land_total = first[:, channels : channels + 1]
    hac_v[...] = first[:, :channels] * ((B + 1) / land_total)
    mean = second[0:1, channels:] / land_total[0:1, :]
    weighed = jnp.sum(wgt_v[...] * mean, axis=1, keepdims=True)
    jacobian = -second[:, :channels] / land_total
    gradient = 2.0 * jnp.sum(jacobian * weighed, axis=0, keepdims=True)
    new_v[...] = coef_v[...] - step_rate * gradient

    def drain(c, carry):
        out_copy(c).wait()

        @pl.when(has_left)
        def _():
            to_left(c).wait_send()

        @pl.when(has_right)
        def _():
            to_right(c).wait_send()

        @pl.when(has_upper)
        def _():
            to_upper(c).wait_send()

        @pl.when(has_lower)
        def _():
            to_lower(c).wait_send()

        return carry

    lax.fori_loop(0, n_chunks, drain, 0)


def local(nx, ny, instruments, regressors, outcome, land_mask, coefficients, weighting):
    channels, rows, cols = instruments.shape
    n_chunks = channels // CH
    pieces = channels // 8
    own = 2 * pieces // nx
    any_spec = pl.BlockSpec(memory_space=pl.ANY)
    vmem_spec = pl.BlockSpec(memory_space=pltpu.VMEM)
    dma = pltpu.SemaphoreType.DMA
    smoothed, hac_cov, new_coefficients = pl.pallas_call(
        functools.partial(kernel, nx, ny),
        out_shape=(
            jax.ShapeDtypeStruct((channels, rows, cols), BF16),
            jax.ShapeDtypeStruct((channels, channels), F32),
            jax.ShapeDtypeStruct((1, channels), F32),
        ),
        in_specs=[any_spec] * 4 + [pl.BlockSpec(memory_space=pltpu.SMEM), vmem_spec, vmem_spec],
        out_specs=(any_spec, vmem_spec, vmem_spec),
        scratch_shapes=[
            pltpu.VMEM((channels, rows, cols), BF16),
            pltpu.VMEM((channels, rows, cols), BF16),
            pltpu.VMEM((rows, cols), F32),
            pltpu.VMEM((rows, cols), jnp.int32),
            pltpu.VMEM((channels, cols), F32),
            pltpu.VMEM((rows, cols), F32),
            pltpu.VMEM((rows, cols), BF16),
            pltpu.VMEM((channels, rows, cols), BF16),
            pltpu.VMEM((channels, rows // 2, 128), BF16),
            pltpu.VMEM((channels, rows // 2, 128), BF16),
            pltpu.VMEM((channels, rows // 2, 128), BF16),
            pltpu.VMEM((channels, rows // 2, 128), BF16),
            pltpu.VMEM((channels, 2 * rows, cols), BF16),
            pltpu.VMEM((channels, rows, cols), BF16),
            pltpu.VMEM((2 * cols, cols), BF16),
            pltpu.VMEM((2 * cols, cols), BF16),
            pltpu.VMEM((rows, 2 * rows), BF16),
            pltpu.VMEM((channels * SUB, GROUP * SUB), F32),
            pltpu.VMEM((channels, 128), F32),
            pltpu.VMEM((channels, 128), F32),
            pltpu.VMEM((channels, cols), F32),
            pltpu.VMEM((2 * pieces, 8, 128), F32),
            pltpu.VMEM((nx, own, 8, 128), F32),
            pltpu.VMEM((own, 8, 128), F32),
            pltpu.VMEM((ny, own, 8, 128), F32),
            pltpu.VMEM((own, 8, 128), F32),
            pltpu.VMEM((2 * pieces, 8, 128), F32),
            dma((2,)),
            dma((4,)),
            dma((channels // GROUP,)),
        ]
        + [dma((n_chunks,))] * 9
        + [dma((3,)), dma((3,))],
        compiler_params=pltpu.CompilerParams(
            collective_id=0, has_side_effects=True, vmem_limit_bytes=48 * 1024 * 1024
        ),
        cost_estimate=pl.CostEstimate(flops=5 * 10**9, bytes_accessed=13 * 2**20, transcendentals=0),
    )(
        instruments,
        regressors,
        outcome,
        land_mask,
        coefficients,
        coefficients.reshape(1, channels),
        weighting,
    )
    return smoothed, hac_cov, new_coefficients.reshape(channels)


def solution(mesh):
    placed = (P(None, "gx", "gy"), P(None, "gx", "gy"), P("gx", "gy"), P("gx", "gy"), P(), P())
    return jax.shard_map(
        functools.partial(local, mesh.shape["gx"], mesh.shape["gy"]),
        mesh=mesh,
        in_specs=placed,
        out_specs=(P(None, "gx", "gy"), P(), P()),
        check_vma=False,
    )
```

```python
import functools

import jax
import jax.numpy as jnp
from jax import lax
from jax.experimental import pallas as pl
from jax.experimental.pallas import tpu as pltpu
from jax.sharding import PartitionSpec as P

B = 64
step_rate = 0.05
MESH = pl.DeviceIdType.MESH
F32 = jnp.float32
BF16 = jnp.bfloat16
CH = 8
SUB = 8
LAG = 1
COV_BLOCKS = ((0, 32), (32, 16), (48, 16))
JAC_BLOCK = 32
TAIL = 32


def iota(shape, dim):
    return lax.broadcasted_iota(jnp.int32, shape, dim)


def dot(a, b):
    return lax.dot_general(a, b, (((1,), (0,)), ((), ())), preferred_element_type=F32)


def dot_t(a, b):
    return lax.dot_general(a, b, (((1,), (1,)), ((), ())), preferred_element_type=F32)


def wide(ref, *at):
    return jnp.concatenate([ref[(0, *at)], ref[(1, *at)]], axis=-1)


def put_wide(ref, value):
    ref[0] = value[:, :128]
    ref[1] = value[:, 128:]


def hat(distance):
    return jnp.maximum(B + 1 - jnp.abs(distance), 0).astype(F32).astype(BF16)


def kernel(
    nx,
    ny,
    inst_h,
    reg_h,
    outcome_h,
    land_h,
    coef_h,
    sm,
    total_v,
    tail_v,
    inst,
    reg,
    outcome,
    land,
    coef_s,
    coefs,
    weighted,
    land_float,
    mom,
    inst_b,
    reg_b,
    send_l,
    send_r,
    y_l,
    y_r,
    rows_sm,
    sm_b,
    w_top,
    w_bot,
    w_col,
    acc_cov,
    acc_jac,
    cov,
    cov_tail,
    jac,
    sums,
    part,
    got1,
    sum1,
    got2,
    sum2,
    got3,
    tile,
    got4,
    sum4,
    got5,
    in_sem,
    reg_sem,
    inst_sem,
    yl_send,
    yl_recv,
    yr_send,
    yr_recv,
    zt_send,
    zt_recv,
    zb_send,
    zb_recv,
    ar_send,
    ar_recv,
):
    gx = lax.axis_index("gx")
    gy = lax.axis_index("gy")
    channels, rows, cols = inst.shape
    half = rows // 2
    n_chunks = channels // CH
    reg_rows = rows // 4
    blocks = rows // SUB

    def outcome_copy():
        return pltpu.make_async_copy(outcome_h, outcome, in_sem.at[0])

    def land_copy():
        return pltpu.make_async_copy(land_h, land, in_sem.at[1])

    def coef_copy():
        return pltpu.make_async_copy(coef_h, coef_s, in_sem.at[2])

    def reg_copy(r):
        at = pl.ds(pl.multiple_of(r * reg_rows, reg_rows), reg_rows)
        return pltpu.make_async_copy(reg_h.at[:, at, :], reg.at[:, at, :], reg_sem.at[r])

    def inst_copy(c):
        at = pl.ds(c * CH, CH)
        return pltpu.make_async_copy(inst_h.at[at], inst.at[at], inst_sem.at[c])

    coef_copy().start()
    reg_copy(0).start()
    outcome_copy().start()
    land_copy().start()
    for r in range(1, 4):
        reg_copy(r).start()
    for c in range(n_chunks):
        inst_copy(c).start()

    barrier = pltpu.get_barrier_semaphore()

    def greet_x(o, carry):
        pl.semaphore_signal(barrier, inc=1, device_id=((gx + o) % nx, gy), device_id_type=MESH)
        return carry

    def greet_y(o, carry):
        pl.semaphore_signal(barrier, inc=1, device_id=(gx, (gy + o) % ny), device_id_type=MESH)
        return carry

    lax.fori_loop(1, nx, greet_x, 0)
    lax.fori_loop(1, ny, greet_y, 0)

    src = iota((cols, cols), 0)
    dst = iota((cols, cols), 1)
    own_band = hat(src - dst)
    low = src % half
    side = jnp.where(src < 2 * half, low - half, low + cols)
    ramp = jnp.maximum(B + 1 - jnp.abs(side - dst), 0).astype(F32)
    is_top = (src // half) % 2 == 0
    put_wide(w_top, jnp.concatenate([own_band, jnp.where(is_top, ramp, 0.0).astype(BF16)], axis=0))
    put_wide(w_bot, jnp.concatenate([own_band, jnp.where(is_top, 0.0, ramp).astype(BF16)], axis=0))
    put_wide(w_col, hat(iota((rows, 2 * rows), 1) - half - iota((rows, 2 * rows), 0)))

    @pl.when(gy == 0)
    def _():
        y_l[...] = jnp.zeros_like(y_l)

    @pl.when(gy == ny - 1)
    def _():
        y_r[...] = jnp.zeros_like(y_r)

    def clear(start):
        def body(k, carry):
            rows_sm[:, k, start : start + half, :] = jnp.zeros((2, half, 128), BF16)
            return carry

        lax.fori_loop(0, channels, body, 0)

    @pl.when(gx == 0)
    def _():
        clear(0)

    @pl.when(gx == nx - 1)
    def _():
        clear(rows + half)

    cov[...] = jnp.zeros_like(cov)
    cov_tail[...] = jnp.zeros_like(cov_tail)
    jac[...] = jnp.zeros_like(jac)
    acc_cov[...] = jnp.zeros_like(acc_cov)
    acc_jac[...] = jnp.zeros_like(acc_jac)

    coef_copy().wait()
    for p in range(channels):
        coefs[p : p + 1, :] = jnp.full((1, cols), coef_s[p], F32)
    coefs[...] = coefs[...].astype(BF16).astype(F32)

    def residuals(r, carry):
        reg_copy(r).wait()
        at = pl.ds(pl.multiple_of(r * reg_rows, reg_rows), reg_rows)

        def add(q, total):
            for u in range(8):
                p = q * 8 + u
                total = total + reg[p, at, :].astype(F32) * coefs[pl.ds(p, 1), :]
            return total

        fitted = lax.fori_loop(0, channels // 8, add, jnp.zeros((reg_rows, cols), F32))

        @pl.when(r == 0)
        def _():
            outcome_copy().wait()
            land_copy().wait()

        here = land[at, :].astype(F32)
        weighted[at, :] = here * (outcome[at, :] - fitted)
        land_float[at, :] = here
        return carry

    lax.fori_loop(0, 4, residuals, 0)

    def chunk_rows(c):
        return pl.ds(pl.multiple_of(c * CH * SUB, CH * SUB), CH * SUB)

    def to_left(c):
        return pltpu.make_async_remote_copy(
            src_ref=send_l.at[:, chunk_rows(c), :],
            dst_ref=y_r.at[:, chunk_rows(c), :],
            send_sem=yl_send.at[c],
            recv_sem=yr_recv.at[c],
            device_id=(gx, gy - 1),
            device_id_type=MESH,
        )

    def to_right(c):
        return pltpu.make_async_remote_copy(
            src_ref=send_r.at[:, chunk_rows(c), :],
            dst_ref=y_l.at[:, chunk_rows(c), :],
            send_sem=yr_send.at[c],
            recv_sem=yl_recv.at[c],
            device_id=(gx, gy + 1),
            device_id_type=MESH,
        )

    def to_upper(c):
        at = pl.ds(c * CH, CH)
        return pltpu.make_async_remote_copy(
            src_ref=rows_sm.at[:, at, half : 2 * half, :],
            dst_ref=rows_sm.at[:, at, 3 * half : 4 * half, :],
            send_sem=zt_send.at[c],
            recv_sem=zb_recv.at[c],
            device_id=(gx - 1, gy),
            device_id_type=MESH,
        )

    def to_lower(c):
        at = pl.ds(c * CH, CH)
        return pltpu.make_async_remote_copy(
            src_ref=rows_sm.at[:, at, 2 * half : 3 * half, :],
            dst_ref=rows_sm.at[:, at, 0:half, :],
            send_sem=zb_send.at[c],
            recv_sem=zt_recv.at[c],
            device_id=(gx + 1, gy),
            device_id_type=MESH,
        )

    has_left, has_right = gy > 0, gy < ny - 1
    has_upper, has_lower = gx > 0, gx < nx - 1

    first_lanes = iota((2 * SUB, 128), 1) < B

    def store_blocked(ref, first_block, at, one, two):
        ref[first_block, at, :] = jnp.concatenate([one[:SUB], two[:SUB]], axis=0).astype(BF16)
        ref[first_block + 1, at, :] = jnp.concatenate([one[SUB:], two[SUB:]], axis=0).astype(BF16)

    def store_wide(ref, first_block, at, one, two):
        for h in range(2):
            lanes = slice(128 * h, 128 * h + 128)
            store_blocked(ref.at[h], first_block, at, one[:, lanes], two[:, lanes])

    def moments(c, carry):
        inst_copy(c).wait()

        def channel_pair(u, inner):
            k = c * CH + 2 * u
            at = pl.ds(pl.multiple_of(k * SUB, 2 * SUB), 2 * SUB)
            for r in range(0, half, 2 * SUB):
                first = r // SUB
                upper, lower = slice(r, r + 2 * SUB), slice(half + r, half + r + 2 * SUB)
                w_upper, w_lower = weighted[upper, :], weighted[lower, :]
                raw = [(inst[k + v, upper, :].astype(F32), inst[k + v, lower, :].astype(F32)) for v in range(2)]
                prods = [(top * w_upper, bot * w_lower) for top, bot in raw]
                store_wide(inst_b, first, at, raw[0][0], raw[1][0])
                store_wide(inst_b, blocks // 2 + first, at, raw[0][1], raw[1][1])
                store_wide(mom, first, at, prods[0][0], prods[1][0])
                store_wide(mom, blocks // 2 + first, at, prods[0][1], prods[1][1])
                left = [
                    jnp.where(first_lanes, top[:, :128], pltpu.roll(bot[:, :128], B, 1)) for top, bot in prods
                ]
                right = [
                    jnp.where(first_lanes, pltpu.roll(top[:, cols - 128 :], B, 1), bot[:, cols - 128 :])
                    for top, bot in prods
                ]
                store_blocked(send_l, first, at, left[0], left[1])
                store_blocked(send_r, first, at, right[0], right[1])
            return inner

        lax.fori_loop(0, CH // 2, channel_pair, 0)

        @pl.when(c == 0)
        def _():
            pl.semaphore_wait(barrier, nx - 1 + ny - 1)

        @pl.when(has_left)
        def _():
            to_left(c).start()

        @pl.when(has_right)
        def _():
            to_right(c).start()

        return carry

    lax.fori_loop(0, n_chunks, moments, 0)

    def block_regressors(u, carry):
        at = pl.ds(pl.multiple_of(2 * u * SUB, 2 * SUB), 2 * SUB)
        for r in range(0, rows, 2 * SUB):
            here = land_float[r : r + 2 * SUB, :]
            one = reg[2 * u, r : r + 2 * SUB, :].astype(F32) * here
            two = reg[2 * u + 1, r : r + 2 * SUB, :].astype(F32) * here
            store_wide(reg_b, r // SUB, at, one, two)
        return carry

    def product(acc, left_ref, left_rows, right_ref, right_rows, b):
        at = (slice(0, left_rows.size), slice(0, right_rows.size))
        lhs = jnp.concatenate([wide(left_ref, b, left_rows), wide(left_ref, b + 1, left_rows)], axis=1)
        rhs = jnp.concatenate([wide(right_ref, b, right_rows), wide(right_ref, b + 1, right_rows)], axis=1)
        acc[at] += dot_t(lhs, rhs)

    def fold(acc, left_count, right_count, first_column):
        at = (slice(0, left_count * SUB), slice(0, right_count * SUB))
        shape = (1, SUB, right_count * SUB)
        kept = jnp.where(iota(shape, 2) % SUB == iota(shape, 1), acc[at].reshape(left_count, SUB, right_count * SUB), 0.0)
        kept = jnp.sum(kept, axis=1)
        pick = iota((right_count * SUB, 128), 0) // SUB + first_column == iota((right_count * SUB, 128), 1)
        acc[...] = jnp.zeros_like(acc)
        return lax.dot_general(
            kept,
            pick.astype(F32),
            (((1,), (0,)), ((), ())),
            precision=lax.Precision.HIGHEST,
            preferred_element_type=F32,
        )

    def jac_part(first, b):
        at = pl.ds(pl.multiple_of(first * SUB, JAC_BLOCK * SUB), JAC_BLOCK * SUB)
        product(acc_jac, inst_b, pl.ds(0, channels * SUB), reg_b, at, b)

    def jac_fold(first):
        jac[...] += fold(acc_jac, channels, JAC_BLOCK, first)

    def cov_part(first, count, b):
        left = pl.ds(first * SUB, (channels - first) * SUB)
        product(acc_cov, mom, left, sm_b, pl.ds(first * SUB, count * SUB), b)

    def cov_fold(ref, first, count):
        ref[first:, :] += fold(acc_cov, channels - first, count, first)

    def moment_sums(b):
        if b == 0:
            sums[...] = jnp.zeros_like(sums)
        sums[...] += wide(mom, b).astype(F32) + wide(mom, b + 1).astype(F32)

    def smooth_rows(c):
        @pl.when(has_left)
        def _():
            to_right(c).wait_recv()

        @pl.when(has_right)
        def _():
            to_left(c).wait_recv()

        at = chunk_rows(c)
        for start, weights in ((0, w_top), (half, w_bot)):
            lhs = jnp.concatenate(
                [
                    jnp.concatenate([wide(mom, start // SUB + b, at), y_l[b, at, :], y_r[b, at, :]], axis=1)
                    for b in range(half // SUB)
                ],
                axis=0,
            )
            total = dot(lhs, wide(weights)) * (1.0 / (B + 1))
            for b in range(0, half // SUB, 2):
                for u in range(CH):
                    one = total[(b * CH + u) * SUB : (b * CH + u + 1) * SUB]
                    two = total[((b + 1) * CH + u) * SUB : ((b + 1) * CH + u + 1) * SUB]
                    place = half + start + b * SUB
                    both = jnp.concatenate([one, two], axis=0).astype(BF16)
                    rows_sm[0, c * CH + u, place : place + 2 * SUB, :] = both[:, :128]
                    rows_sm[1, c * CH + u, place : place + 2 * SUB, :] = both[:, 128:]

        @pl.when(has_upper)
        def _():
            to_upper(c).start()

        @pl.when(has_lower)
        def _():
            to_lower(c).start()

    def smooth_columns(c):
        @pl.when(has_upper)
        def _():
            to_lower(c).wait_recv()

        @pl.when(has_lower)
        def _():
            to_upper(c).wait_recv()

        for u in range(0, CH, 2):
            k = c * CH + u
            pair = [dot(wide(w_col), wide(rows_sm, k + v)) * (1.0 / (B + 1) ** 2) for v in range(2)]
            sm[k] = pair[0].astype(BF16)
            sm[k + 1] = pair[1].astype(BF16)
            at = pl.ds(pl.multiple_of(k * SUB, 2 * SUB), 2 * SUB)
            for r in range(0, rows, 2 * SUB):
                store_wide(sm_b, r // SUB, at, pair[0][r : r + 2 * SUB], pair[1][r : r + 2 * SUB])

    pieces = channels // 8
    own_pieces = 2 * pieces // nx

    def send_all(number, peers, me, copy):
        def send(o, carry):
            copy(number, (me + o) % peers).start()
            return carry

        lax.fori_loop(1, peers, send, 0)

    def land_all(number, landed):
        pltpu.make_async_copy(landed, landed, ar_recv.at[number]).wait()
        pltpu.make_async_copy(landed, landed, ar_send.at[number]).wait()

    def own(g):
        return pl.ds(g * own_pieces, own_pieces)

    def remote(number, src, dst, device):
        return pltpu.make_async_remote_copy(
            src_ref=src,
            dst_ref=dst,
            send_sem=ar_send.at[number],
            recv_sem=ar_recv.at[number],
            device_id=device,
            device_id_type=MESH,
        )

    def scatter(number, g):
        return remote(number, part.at[own(g)], got1.at[gx], (g, gy))

    def across(number, g):
        return remote(number, sum1, got2.at[gy], (gx, g))

    def gather(number, g):
        return remote(number, sum2, got3.at[own(gx)], (g, gy))

    def tail_x(number, g):
        return remote(number, tile, got4.at[gx], (g, gy))

    def tail_y(number, g):
        return remote(number, sum4, got5.at[gy], (gx, g))

    def early_scatter():
        count = jnp.sum(jnp.sum(land_float[...], axis=0, keepdims=True), axis=1, keepdims=True)
        columns = jnp.sum(jnp.sum(sums[...].reshape(channels, SUB, cols), axis=1), axis=1, keepdims=True)
        right_half = iota((channels, 128), 1) >= channels
        as_row = jnp.sum(
            jnp.where(iota((channels, 128), 1) - channels == iota((channels, 128), 0), columns, 0.0),
            axis=0,
            keepdims=True,
        )
        part[0:pieces] = jnp.where(right_half, count, cov[...]).reshape(pieces, 8, 128)
        part[pieces : 2 * pieces] = jnp.where(right_half, as_row, jac[...]).reshape(pieces, 8, 128)
        got1[gx] = part[own(gx)]
        send_all(0, nx, gx, scatter)

    def early_across():
        land_all(0, got1.at[0 : nx - 1])
        sum1[...] = jnp.sum(got1[...], axis=0)
        got2[gy] = sum1[...]
        send_all(1, ny, gy, across)

    def early_gather():
        land_all(1, got2.at[0 : ny - 1])
        sum2[...] = jnp.sum(got2[...], axis=0)
        got3[own(gx)] = sum2[...]
        send_all(2, nx, gx, gather)

    last = n_chunks + LAG - 1

    def pipeline(t, carry):
        @pl.when(t < n_chunks)
        def _():
            smooth_rows(t)

        @pl.when(t == 0)
        def _():
            lax.fori_loop(0, channels // 2, block_regressors, 0)
            for b in range(0, blocks, 2):
                moment_sums(b)

        for g in range(channels // JAC_BLOCK):

            @pl.when(jnp.logical_or(t == 1 + 2 * g, t == 2 + 2 * g))
            def _(g=g):
                for u in range(0, blocks // 2, 2):
                    jac_part(g * JAC_BLOCK, (t - 1 - 2 * g) * (blocks // 2) + u)

            @pl.when(t == 2 + 2 * g)
            def _(g=g):
                jac_fold(g * JAC_BLOCK)

        first, count = COV_BLOCKS[0]
        begin = (first + count) // CH + LAG

        @pl.when(jnp.logical_or(t == begin, t == begin + 1))
        def _(first=first, count=count, begin=begin):
            for u in range(0, blocks // 2, 2):
                cov_part(first, count, (t - begin) * (blocks // 2) + u)

        @pl.when(t == begin + 1)
        def _(first=first, count=count):
            cov_fold(cov, first, count)
            early_scatter()

        first, count = COV_BLOCKS[1]
        begin = (first + count) // CH + LAG

        @pl.when(t == begin)
        def _(first=first, count=count):
            early_across()
            for b in range(0, blocks, 2):
                cov_part(first, count, b)
            cov_fold(cov_tail, first, count)

        @pl.when(t == last)
        def _():
            early_gather()

        @pl.when(t >= LAG)
        def _():
            smooth_columns(t - LAG)

        return carry

    lax.fori_loop(0, last + 1, pipeline, 0)

    first, count = COV_BLOCKS[2]
    for b in range(0, blocks, 2):
        cov_part(first, count, b)
    cov_fold(cov_tail, first, count)

    lane_group = iota((8, 128), 1) // 32
    packed = jnp.zeros((8, 128), F32)
    for g in range((channels - TAIL) // 8):
        piece = cov_tail[TAIL + 8 * g : TAIL + 8 * g + 8, :]
        packed = jnp.where(lane_group == g, pltpu.roll(piece, (32 * g - TAIL) % 128, 1), packed)
    tile[...] = packed
    send_all(3, nx, gx, tail_x)
    got4[gx] = tile[...]

    def drain(c, carry):
        @pl.when(has_left)
        def _():
            to_left(c).wait_send()

        @pl.when(has_right)
        def _():
            to_right(c).wait_send()

        @pl.when(has_upper)
        def _():
            to_upper(c).wait_send()

        @pl.when(has_lower)
        def _():
            to_lower(c).wait_send()

        return carry

    lax.fori_loop(0, n_chunks, drain, 0)
    land_all(2, got3.at[0 : (nx - 1) * own_pieces])
    total_v[...] = got3[...].reshape(2 * channels, 128)

    land_all(3, got4.at[0 : nx - 1])
    sum4[...] = jnp.sum(got4[...], axis=0)
    send_all(4, ny, gy, tail_y)
    got5[gy] = sum4[...]
    land_all(4, got5.at[0 : ny - 1])
    tail_v[...] = jnp.sum(got5[...], axis=0)


def finish(s_in, total_v, tail_v, coef_v, wgt_v, s_out, hac_v, new_v, sem):
    channels = s_in.shape[0]
    share = channels // 16

    def move(c):
        at = pl.ds(c * share, share)
        return pltpu.make_async_copy(s_in.at[at], s_out.at[at], sem.at[c])

    for c in range(16):
        move(c).start()
    first, second = total_v[0:channels, :], total_v[channels : 2 * channels, :]
    land_total = first[:, channels : channels + 1]
    tail = jnp.concatenate([pltpu.roll(tail_v[...], (TAIL - 32 * g) % 128, 1) for g in range((channels - TAIL) // 8)], axis=0)
    bottom = jnp.where(iota(tail.shape, 1) >= TAIL, tail, first[TAIL:, :])
    lower = jnp.concatenate([first[:TAIL, :], bottom], axis=0)[:, :channels]
    row, column = iota((channels, channels), 0), iota((channels, channels), 1)
    held = row >= 0
    for start, count in COV_BLOCKS:
        held = jnp.logical_and(held, jnp.logical_or(column < start, row >= start))
    hac_v[...] = jnp.where(held, lower, lower.T) * ((B + 1) / land_total)
    mean = second[0:1, channels:] / land_total[0:1, :]
    weighed = jnp.sum(wgt_v[...] * mean, axis=1, keepdims=True)
    jacobian = -second[:, :channels] / land_total
    gradient = 2.0 * jnp.sum(jacobian * weighed, axis=0, keepdims=True)
    new_v[...] = coef_v[...] - step_rate * gradient
    for c in range(16):
        move(c).wait()


def local(nx, ny, instruments, regressors, outcome, land_mask, coefficients, weighting):
    channels, rows, cols = instruments.shape
    n_chunks = channels // CH
    pieces = channels // 8
    own = 2 * pieces // nx
    blocks = rows // SUB
    any_spec = pl.BlockSpec(memory_space=pl.ANY)
    in_hbm = functools.partial(pltpu.with_memory_space_constraint, memory_space=pltpu.HBM)
    in_vmem = functools.partial(pltpu.with_memory_space_constraint, memory_space=pltpu.VMEM)
    hbm_spec = pl.BlockSpec(memory_space=pltpu.HBM)
    vmem_spec = pl.BlockSpec(memory_space=pltpu.VMEM)
    dma = pltpu.SemaphoreType.DMA
    blocked = pltpu.VMEM((2, blocks, channels * SUB, 128), BF16)
    edge = pltpu.VMEM((blocks // 2, channels * SUB, 128), BF16)
    smoothed, totals, tail = pl.pallas_call(
        functools.partial(kernel, nx, ny),
        out_shape=(
            pltpu.VMEM((channels, rows, cols), BF16),
            pltpu.VMEM((2 * channels, 128), F32),
            pltpu.VMEM((8, 128), F32),
        ),
        in_specs=[hbm_spec] * 5,
        out_specs=(vmem_spec, vmem_spec, vmem_spec),
        scratch_shapes=[
            pltpu.VMEM((channels, rows, cols), BF16),
            pltpu.VMEM((channels, rows, cols), BF16),
            pltpu.VMEM((rows, cols), F32),
            pltpu.VMEM((rows, cols), jnp.int32),
            pltpu.SMEM((channels,), F32),
            pltpu.VMEM((channels, cols), F32),
            pltpu.VMEM((rows, cols), F32),
            pltpu.VMEM((rows, cols), F32),
            blocked,
            blocked,
            blocked,
            edge,
            edge,
            edge,
            edge,
            pltpu.VMEM((2, channels, 2 * rows, 128), BF16),
            blocked,
            pltpu.VMEM((2, 2 * cols, 128), BF16),
            pltpu.VMEM((2, 2 * cols, 128), BF16),
            pltpu.VMEM((2, rows, 128), BF16),
            pltpu.VMEM((channels * SUB, 32 * SUB), F32),
            pltpu.VMEM((channels * SUB, 32 * SUB), F32),
            pltpu.VMEM((channels, 128), F32),
            pltpu.VMEM((channels, 128), F32),
            pltpu.VMEM((channels, 128), F32),
            pltpu.VMEM((channels * SUB, cols), F32),
            pltpu.VMEM((2 * pieces, 8, 128), F32),
            pltpu.VMEM((nx, own, 8, 128), F32),
            pltpu.VMEM((own, 8, 128), F32),
            pltpu.VMEM((ny, own, 8, 128), F32),
            pltpu.VMEM((own, 8, 128), F32),
            pltpu.VMEM((2 * pieces, 8, 128), F32),
            pltpu.VMEM((8, 128), F32),
            pltpu.VMEM((nx, 8, 128), F32),
            pltpu.VMEM((8, 128), F32),
            pltpu.VMEM((ny, 8, 128), F32),
            dma((3,)),
            dma((4,)),
            dma((n_chunks,)),
        ]
        + [dma((n_chunks,))] * 8
        + [dma((5,)), dma((5,))],
        compiler_params=pltpu.CompilerParams(
            collective_id=0, has_side_effects=True, vmem_limit_bytes=42 * 1024 * 1024
        ),
        cost_estimate=pl.CostEstimate(flops=5 * 10**9, bytes_accessed=13 * 2**20, transcendentals=0),
    )(*map(in_hbm, (instruments, regressors, outcome, land_mask, coefficients)))
    smoothed, hac_cov, new_coefficients = pl.pallas_call(
        finish,
        out_shape=(
            jax.ShapeDtypeStruct((channels, rows, cols), BF16),
            jax.ShapeDtypeStruct((channels, channels), F32),
            jax.ShapeDtypeStruct((1, channels), F32),
        ),
        in_specs=[vmem_spec] * 5,
        out_specs=(any_spec, vmem_spec, vmem_spec),
        scratch_shapes=[dma((16,))],
        compiler_params=pltpu.CompilerParams(vmem_limit_bytes=4 * 1024 * 1024),
        cost_estimate=pl.CostEstimate(flops=10**6, bytes_accessed=8 * 2**20, transcendentals=0),
    )(in_vmem(smoothed), in_vmem(totals), in_vmem(tail), coefficients.reshape(1, channels), weighting)
    return smoothed, hac_cov, new_coefficients.reshape(channels)


def solution(mesh):
    placed = (P(None, "gx", "gy"), P(None, "gx", "gy"), P("gx", "gy"), P("gx", "gy"), P(), P())
    return jax.shard_map(
        functools.partial(local, mesh.shape["gx"], mesh.shape["gy"]),
        mesh=mesh,
        in_specs=placed,
        out_specs=(P(None, "gx", "gy"), P(), P()),
        check_vma=False,
    )
```

```python
import functools

import jax
import jax.numpy as jnp
from jax import lax
from jax.experimental import pallas as pl
from jax.experimental.pallas import tpu as pltpu
from jax.sharding import PartitionSpec as P

B = 64
step_rate = 0.05
MESH = pl.DeviceIdType.MESH
F32 = jnp.float32
BF16 = jnp.bfloat16
CH = 8
SUB = 8
AHEAD = 2
LAG = 1
COV_BLOCKS = ((0, 32), (32, 16), (48, 16))
JAC_BLOCK = 32
TAIL = 32


def iota(shape, dim):
    return lax.broadcasted_iota(jnp.int32, shape, dim)


def dot(a, b):
    return lax.dot_general(a, b, (((1,), (0,)), ((), ())), preferred_element_type=F32)


def dot_t(a, b):
    return lax.dot_general(a, b, (((1,), (1,)), ((), ())), preferred_element_type=F32)


def wide(ref, *at):
    return jnp.concatenate([ref[(0, *at)], ref[(1, *at)]], axis=-1)


def put_wide(ref, value):
    ref[0] = value[:, :128]
    ref[1] = value[:, 128:]


def hat(distance):
    return jnp.maximum(B + 1 - jnp.abs(distance), 0).astype(F32).astype(BF16)


def kernel(
    nx,
    ny,
    inst_h,
    reg_h,
    outcome_h,
    land_h,
    coef_h,
    sm,
    total_v,
    tail_v,
    inst,
    reg,
    outcome,
    land,
    coef_s,
    coefs,
    weighted,
    land_float,
    mom,
    inst_b,
    reg_b,
    send_l,
    send_r,
    y_l,
    y_r,
    rows_sm,
    sm_b,
    w_top,
    w_bot,
    w_col,
    acc_cov,
    acc_jac,
    cov,
    cov_tail,
    jac,
    sums,
    part,
    got1,
    sum1,
    got2,
    sum2,
    got3,
    tile,
    got4,
    sum4,
    got5,
    in_sem,
    reg_sem,
    inst_sem,
    yl_send,
    yl_recv,
    yr_send,
    yr_recv,
    zt_send,
    zt_recv,
    zb_send,
    zb_recv,
    ar_send,
    ar_recv,
):
    gx = lax.axis_index("gx")
    gy = lax.axis_index("gy")
    channels, rows, cols = inst.shape
    half = rows // 2
    n_chunks = channels // CH
    reg_rows = rows // 4
    blocks = rows // SUB

    def outcome_copy():
        return pltpu.make_async_copy(outcome_h, outcome, in_sem.at[0])

    def land_copy():
        return pltpu.make_async_copy(land_h, land, in_sem.at[1])

    def coef_copy():
        return pltpu.make_async_copy(coef_h, coef_s, in_sem.at[2])

    def reg_copy(r):
        at = pl.ds(pl.multiple_of(r * reg_rows, reg_rows), reg_rows)
        return pltpu.make_async_copy(reg_h.at[:, at, :], reg.at[:, at, :], reg_sem.at[r])

    def inst_copy(c):
        at = pl.ds(c * CH, CH)
        return pltpu.make_async_copy(inst_h.at[at], inst.at[at], inst_sem.at[c])

    coef_copy().start()
    reg_copy(0).start()
    outcome_copy().start()
    land_copy().start()
    for r in range(1, 4):
        reg_copy(r).start()
    for c in range(n_chunks):
        inst_copy(c).start()

    barrier = pltpu.get_barrier_semaphore()

    def greet_x(o, carry):
        pl.semaphore_signal(barrier, inc=1, device_id=((gx + o) % nx, gy), device_id_type=MESH)
        return carry

    def greet_y(o, carry):
        pl.semaphore_signal(barrier, inc=1, device_id=(gx, (gy + o) % ny), device_id_type=MESH)
        return carry

    lax.fori_loop(1, nx, greet_x, 0)
    lax.fori_loop(1, ny, greet_y, 0)

    src = iota((cols, cols), 0)
    dst = iota((cols, cols), 1)
    own_band = hat(src - dst)
    low = src % half
    side = jnp.where(src < 2 * half, low - half, low + cols)
    ramp = jnp.maximum(B + 1 - jnp.abs(side - dst), 0).astype(F32)
    is_top = (src // half) % 2 == 0
    put_wide(w_top, jnp.concatenate([own_band, jnp.where(is_top, ramp, 0.0).astype(BF16)], axis=0))
    put_wide(w_bot, jnp.concatenate([own_band, jnp.where(is_top, 0.0, ramp).astype(BF16)], axis=0))
    put_wide(w_col, hat(iota((rows, 2 * rows), 1) - half - iota((rows, 2 * rows), 0)))

    @pl.when(gy == 0)
    def _():
        y_l[...] = jnp.zeros_like(y_l)

    @pl.when(gy == ny - 1)
    def _():
        y_r[...] = jnp.zeros_like(y_r)

    def clear(start):
        def body(k, carry):
            rows_sm[:, k, start : start + half, :] = jnp.zeros((2, half, 128), BF16)
            return carry

        lax.fori_loop(0, channels, body, 0)

    @pl.when(gx == 0)
    def _():
        clear(0)

    @pl.when(gx == nx - 1)
    def _():
        clear(rows + half)

    cov[...] = jnp.zeros_like(cov)
    cov_tail[...] = jnp.zeros_like(cov_tail)
    jac[...] = jnp.zeros_like(jac)
    acc_cov[...] = jnp.zeros_like(acc_cov)
    acc_jac[...] = jnp.zeros_like(acc_jac)

    coef_copy().wait()
    for p in range(channels):
        coefs[p] = jnp.full((SUB, 128), coef_s[p], F32)
    coefs[...] = coefs[...].astype(BF16).astype(F32)

    def residuals(r, carry):
        reg_copy(r).wait()
        at = pl.ds(pl.multiple_of(r * reg_rows, reg_rows), reg_rows)

        def add(q, total):
            for u in range(8):
                p = q * 8 + u
                one = jnp.concatenate([coefs[p]] * (cols // 128), axis=1)
                total = total + reg[p, at, :].astype(F32) * jnp.concatenate([one] * (reg_rows // SUB), axis=0)
            return total

        fitted = lax.fori_loop(0, channels // 8, add, jnp.zeros((reg_rows, cols), F32))

        @pl.when(r == 0)
        def _():
            outcome_copy().wait()
            land_copy().wait()

        here = land[at, :].astype(F32)
        weighted[at, :] = here * (outcome[at, :] - fitted)
        land_float[at, :] = here
        return carry

    lax.fori_loop(0, 4, residuals, 0)

    def chunk_rows(c):
        return pl.ds(pl.multiple_of(c * CH * SUB, CH * SUB), CH * SUB)

    def to_left(c):
        return pltpu.make_async_remote_copy(
            src_ref=send_l.at[:, chunk_rows(c), :],
            dst_ref=y_r.at[:, chunk_rows(c), :],
            send_sem=yl_send.at[c],
            recv_sem=yr_recv.at[c],
            device_id=(gx, gy - 1),
            device_id_type=MESH,
        )

    def to_right(c):
        return pltpu.make_async_remote_copy(
            src_ref=send_r.at[:, chunk_rows(c), :],
            dst_ref=y_l.at[:, chunk_rows(c), :],
            send_sem=yr_send.at[c],
            recv_sem=yl_recv.at[c],
            device_id=(gx, gy + 1),
            device_id_type=MESH,
        )

    def to_upper(c):
        at = pl.ds(c * CH, CH)
        return pltpu.make_async_remote_copy(
            src_ref=rows_sm.at[:, at, half : 2 * half, :],
            dst_ref=rows_sm.at[:, at, 3 * half : 4 * half, :],
            send_sem=zt_send.at[c],
            recv_sem=zb_recv.at[c],
            device_id=(gx - 1, gy),
            device_id_type=MESH,
        )

    def to_lower(c):
        at = pl.ds(c * CH, CH)
        return pltpu.make_async_remote_copy(
            src_ref=rows_sm.at[:, at, 2 * half : 3 * half, :],
            dst_ref=rows_sm.at[:, at, 0:half, :],
            send_sem=zb_send.at[c],
            recv_sem=zt_recv.at[c],
            device_id=(gx + 1, gy),
            device_id_type=MESH,
        )

    has_left, has_right = gy > 0, gy < ny - 1
    has_upper, has_lower = gx > 0, gx < nx - 1

    def send_edges(c):
        @pl.when(has_left)
        def _():
            to_left(c).start()

        @pl.when(has_right)
        def _():
            to_right(c).start()

    first_lanes = iota((2 * SUB, 128), 1) < B

    def store_blocked(ref, first_block, at, one, two):
        ref[first_block, at, :] = jnp.concatenate([one[:SUB], two[:SUB]], axis=0).astype(BF16)
        ref[first_block + 1, at, :] = jnp.concatenate([one[SUB:], two[SUB:]], axis=0).astype(BF16)

    def store_wide(ref, first_block, at, one, two):
        for h in range(2):
            lanes = slice(128 * h, 128 * h + 128)
            store_blocked(ref.at[h], first_block, at, one[:, lanes], two[:, lanes])

    def moments(c, carry):
        inst_copy(c).wait()

        def channel_pair(u, inner):
            k = c * CH + 2 * u
            at = pl.ds(pl.multiple_of(k * SUB, 2 * SUB), 2 * SUB)
            for r in range(0, half, 2 * SUB):
                first = r // SUB
                upper, lower = slice(r, r + 2 * SUB), slice(half + r, half + r + 2 * SUB)
                w_upper, w_lower = weighted[upper, :], weighted[lower, :]
                raw = [(inst[k + v, upper, :].astype(F32), inst[k + v, lower, :].astype(F32)) for v in range(2)]
                prods = [(top * w_upper, bot * w_lower) for top, bot in raw]
                store_wide(inst_b, first, at, raw[0][0], raw[1][0])
                store_wide(inst_b, blocks // 2 + first, at, raw[0][1], raw[1][1])
                store_wide(mom, first, at, prods[0][0], prods[1][0])
                store_wide(mom, blocks // 2 + first, at, prods[0][1], prods[1][1])
                left = [
                    jnp.where(first_lanes, top[:, :128], pltpu.roll(bot[:, :128], B, 1)) for top, bot in prods
                ]
                right = [
                    jnp.where(first_lanes, pltpu.roll(top[:, cols - 128 :], B, 1), bot[:, cols - 128 :])
                    for top, bot in prods
                ]
                store_blocked(send_l, first, at, left[0], left[1])
                store_blocked(send_r, first, at, right[0], right[1])
            return inner

        lax.fori_loop(0, CH // 2, channel_pair, 0)

        @pl.when(c == 0)
        def _():
            pl.semaphore_wait(barrier, nx - 1 + ny - 1)

        @pl.when(c < AHEAD)
        def _():
            send_edges(c)

        return carry

    lax.fori_loop(0, n_chunks, moments, 0)

    def block_regressors(u, carry):
        at = pl.ds(pl.multiple_of(2 * u * SUB, 2 * SUB), 2 * SUB)
        for r in range(0, rows, 2 * SUB):
            here = land_float[r : r + 2 * SUB, :]
            one = reg[2 * u, r : r + 2 * SUB, :].astype(F32) * here
            two = reg[2 * u + 1, r : r + 2 * SUB, :].astype(F32) * here
            store_wide(reg_b, r // SUB, at, one, two)
        return carry

    def product(acc, left_ref, left_rows, right_ref, right_rows, b):
        at = (slice(0, left_rows.size), slice(0, right_rows.size))
        lhs = jnp.concatenate([wide(left_ref, b, left_rows), wide(left_ref, b + 1, left_rows)], axis=1)
        rhs = jnp.concatenate([wide(right_ref, b, right_rows), wide(right_ref, b + 1, right_rows)], axis=1)
        acc[at] += dot_t(lhs, rhs)

    def fold(acc, left_count, right_count, first_column):
        at = (slice(0, left_count * SUB), slice(0, right_count * SUB))
        shape = (1, SUB, right_count * SUB)
        kept = jnp.where(iota(shape, 2) % SUB == iota(shape, 1), acc[at].reshape(left_count, SUB, right_count * SUB), 0.0)
        kept = jnp.sum(kept, axis=1)
        pick = iota((right_count * SUB, 128), 0) // SUB + first_column == iota((right_count * SUB, 128), 1)
        acc[...] = jnp.zeros_like(acc)
        return lax.dot_general(
            kept,
            pick.astype(F32),
            (((1,), (0,)), ((), ())),
            precision=lax.Precision.HIGHEST,
            preferred_element_type=F32,
        )

    def jac_part(first, b):
        at = pl.ds(pl.multiple_of(first * SUB, JAC_BLOCK * SUB), JAC_BLOCK * SUB)
        product(acc_jac, inst_b, pl.ds(0, channels * SUB), reg_b, at, b)

    def jac_fold(first):
        jac[...] += fold(acc_jac, channels, JAC_BLOCK, first)

    def cov_part(first, count, b):
        left = pl.ds(first * SUB, (channels - first) * SUB)
        product(acc_cov, mom, left, sm_b, pl.ds(first * SUB, count * SUB), b)

    def cov_fold(ref, first, count):
        ref[first:, :] += fold(acc_cov, channels - first, count, first)

    def moment_sums(b):
        if b == 0:
            sums[...] = jnp.zeros_like(sums)
        sums[...] += wide(mom, b).astype(F32) + wide(mom, b + 1).astype(F32)

    def smooth_rows(c):
        @pl.when(has_left)
        def _():
            to_right(c).wait_recv()

        @pl.when(has_right)
        def _():
            to_left(c).wait_recv()

        at = chunk_rows(c)
        for start, weights in ((0, w_top), (half, w_bot)):
            lhs = jnp.concatenate(
                [
                    jnp.concatenate([wide(mom, start // SUB + b, at), y_l[b, at, :], y_r[b, at, :]], axis=1)
                    for b in range(half // SUB)
                ],
                axis=0,
            )
            total = dot(lhs, wide(weights)) * (1.0 / (B + 1))
            for b in range(0, half // SUB, 2):
                for u in range(CH):
                    one = total[(b * CH + u) * SUB : (b * CH + u + 1) * SUB]
                    two = total[((b + 1) * CH + u) * SUB : ((b + 1) * CH + u + 1) * SUB]
                    place = half + start + b * SUB
                    both = jnp.concatenate([one, two], axis=0).astype(BF16)
                    rows_sm[0, c * CH + u, place : place + 2 * SUB, :] = both[:, :128]
                    rows_sm[1, c * CH + u, place : place + 2 * SUB, :] = both[:, 128:]

        @pl.when(has_upper)
        def _():
            to_upper(c).start()

        @pl.when(has_lower)
        def _():
            to_lower(c).start()

    def smooth_columns(c):
        @pl.when(has_upper)
        def _():
            to_lower(c).wait_recv()

        @pl.when(has_lower)
        def _():
            to_upper(c).wait_recv()

        for u in range(0, CH, 2):
            k = c * CH + u
            pair = [dot(wide(w_col), wide(rows_sm, k + v)) * (1.0 / (B + 1) ** 2) for v in range(2)]
            sm[k] = pair[0].astype(BF16)
            sm[k + 1] = pair[1].astype(BF16)
            at = pl.ds(pl.multiple_of(k * SUB, 2 * SUB), 2 * SUB)
            for r in range(0, rows, 2 * SUB):
                store_wide(sm_b, r // SUB, at, pair[0][r : r + 2 * SUB], pair[1][r : r + 2 * SUB])

    pieces = channels // 8
    own_pieces = 2 * pieces // nx

    def send_all(number, peers, me, copy):
        def send(o, carry):
            copy(number, (me + o) % peers).start()
            return carry

        lax.fori_loop(1, peers, send, 0)

    def land_all(number, landed):
        pltpu.make_async_copy(landed, landed, ar_recv.at[number]).wait()
        pltpu.make_async_copy(landed, landed, ar_send.at[number]).wait()

    def own(g):
        return pl.ds(g * own_pieces, own_pieces)

    def remote(number, src, dst, device):
        return pltpu.make_async_remote_copy(
            src_ref=src,
            dst_ref=dst,
            send_sem=ar_send.at[number],
            recv_sem=ar_recv.at[number],
            device_id=device,
            device_id_type=MESH,
        )

    def scatter(number, g):
        return remote(number, part.at[own(g)], got1.at[gx], (g, gy))

    def across(number, g):
        return remote(number, sum1, got2.at[gy], (gx, g))

    def gather(number, g):
        return remote(number, sum2, got3.at[own(gx)], (g, gy))

    def tail_x(number, g):
        return remote(number, tile, got4.at[gx], (g, gy))

    def tail_y(number, g):
        return remote(number, sum4, got5.at[gy], (gx, g))

    def early_scatter():
        count = jnp.sum(jnp.sum(land_float[...], axis=0, keepdims=True), axis=1, keepdims=True)
        columns = jnp.sum(jnp.sum(sums[...].reshape(channels, SUB, cols), axis=1), axis=1, keepdims=True)
        right_half = iota((channels, 128), 1) >= channels
        as_row = jnp.sum(
            jnp.where(iota((channels, 128), 1) - channels == iota((channels, 128), 0), columns, 0.0),
            axis=0,
            keepdims=True,
        )
        part[0:pieces] = jnp.where(right_half, count, cov[...]).reshape(pieces, 8, 128)
        part[pieces : 2 * pieces] = jnp.where(right_half, as_row, jac[...]).reshape(pieces, 8, 128)
        got1[gx] = part[own(gx)]
        send_all(0, nx, gx, scatter)

    def early_across():
        land_all(0, got1.at[0 : nx - 1])
        sum1[...] = jnp.sum(got1[...], axis=0)
        got2[gy] = sum1[...]
        send_all(1, ny, gy, across)

    def early_gather():
        land_all(1, got2.at[0 : ny - 1])
        sum2[...] = jnp.sum(got2[...], axis=0)
        got3[own(gx)] = sum2[...]
        send_all(2, nx, gx, gather)

    last = n_chunks + LAG - 1

    def pipeline(t, carry):
        @pl.when(t < n_chunks)
        def _():
            smooth_rows(t)

        @pl.when(t + AHEAD < n_chunks)
        def _():
            send_edges(t + AHEAD)

        @pl.when(t == 0)
        def _():
            lax.fori_loop(0, channels // 2, block_regressors, 0)
            for b in range(0, blocks, 2):
                moment_sums(b)

        for g in range(channels // JAC_BLOCK):

            @pl.when(jnp.logical_or(t == 1 + 2 * g, t == 2 + 2 * g))
            def _(g=g):
                for u in range(0, blocks // 2, 2):
                    jac_part(g * JAC_BLOCK, (t - 1 - 2 * g) * (blocks // 2) + u)

            @pl.when(t == 2 + 2 * g)
            def _(g=g):
                jac_fold(g * JAC_BLOCK)

        first, count = COV_BLOCKS[0]
        begin = (first + count) // CH + LAG

        @pl.when(jnp.logical_or(t == begin, t == begin + 1))
        def _(first=first, count=count, begin=begin):
            for u in range(0, blocks // 2, 2):
                cov_part(first, count, (t - begin) * (blocks // 2) + u)

        @pl.when(t == begin + 1)
        def _(first=first, count=count):
            cov_fold(cov, first, count)
            early_scatter()

        first, count = COV_BLOCKS[1]
        begin = (first + count) // CH + LAG

        @pl.when(t == begin)
        def _(first=first, count=count):
            early_across()
            for b in range(0, blocks, 2):
                cov_part(first, count, b)
            cov_fold(cov_tail, first, count)

        @pl.when(t == last)
        def _():
            early_gather()

        @pl.when(t >= LAG)
        def _():
            smooth_columns(t - LAG)

        return carry

    lax.fori_loop(0, last + 1, pipeline, 0)

    first, count = COV_BLOCKS[2]
    for b in range(0, blocks, 2):
        cov_part(first, count, b)
    cov_fold(cov_tail, first, count)

    lane_group = iota((8, 128), 1) // 32
    packed = jnp.zeros((8, 128), F32)
    for g in range((channels - TAIL) // 8):
        piece = cov_tail[TAIL + 8 * g : TAIL + 8 * g + 8, :]
        packed = jnp.where(lane_group == g, pltpu.roll(piece, (32 * g - TAIL) % 128, 1), packed)
    tile[...] = packed
    send_all(3, nx, gx, tail_x)
    got4[gx] = tile[...]

    def drain(c, carry):
        @pl.when(has_left)
        def _():
            to_left(c).wait_send()

        @pl.when(has_right)
        def _():
            to_right(c).wait_send()

        @pl.when(has_upper)
        def _():
            to_upper(c).wait_send()

        @pl.when(has_lower)
        def _():
            to_lower(c).wait_send()

        return carry

    lax.fori_loop(0, n_chunks, drain, 0)
    land_all(2, got3.at[0 : (nx - 1) * own_pieces])
    total_v[...] = got3[...].reshape(2 * channels, 128)

    land_all(3, got4.at[0 : nx - 1])
    sum4[...] = jnp.sum(got4[...], axis=0)
    send_all(4, ny, gy, tail_y)
    got5[gy] = sum4[...]
    land_all(4, got5.at[0 : ny - 1])
    tail_v[...] = jnp.sum(got5[...], axis=0)


def finish(s_in, total_v, tail_v, coef_v, wgt_v, s_out, hac_v, new_v, sem):
    channels = s_in.shape[0]
    share = channels // 4

    def move(c):
        at = pl.ds(c * share, share)
        return pltpu.make_async_copy(s_in.at[at], s_out.at[at], sem.at[c])

    for c in range(4):
        move(c).start()
    first, second = total_v[0:channels, :], total_v[channels : 2 * channels, :]
    land_total = first[:, channels : channels + 1]
    tail = jnp.concatenate([pltpu.roll(tail_v[...], (TAIL - 32 * g) % 128, 1) for g in range((channels - TAIL) // 8)], axis=0)
    bottom = jnp.where(iota(tail.shape, 1) >= TAIL, tail, first[TAIL:, :])
    lower = jnp.concatenate([first[:TAIL, :], bottom], axis=0)[:, :channels]
    row, column = iota((channels, channels), 0), iota((channels, channels), 1)
    held = row >= 0
    for start, count in COV_BLOCKS:
        held = jnp.logical_and(held, jnp.logical_or(column < start, row >= start))
    hac_v[...] = jnp.where(held, lower, lower.T) * ((B + 1) / land_total)
    mean = second[0:1, channels:] / land_total[0:1, :]
    weighed = jnp.sum(wgt_v[...] * mean, axis=1, keepdims=True)
    jacobian = -second[:, :channels] / land_total
    gradient = 2.0 * jnp.sum(jacobian * weighed, axis=0, keepdims=True)
    new_v[...] = coef_v[...] - step_rate * gradient
    for c in range(4):
        move(c).wait()


def local(nx, ny, instruments, regressors, outcome, land_mask, coefficients, weighting):
    channels, rows, cols = instruments.shape
    n_chunks = channels // CH
    pieces = channels // 8
    own = 2 * pieces // nx
    blocks = rows // SUB
    any_spec = pl.BlockSpec(memory_space=pl.ANY)
    in_hbm = functools.partial(pltpu.with_memory_space_constraint, memory_space=pltpu.HBM)
    in_vmem = functools.partial(pltpu.with_memory_space_constraint, memory_space=pltpu.VMEM)
    hbm_spec = pl.BlockSpec(memory_space=pltpu.HBM)
    vmem_spec = pl.BlockSpec(memory_space=pltpu.VMEM)
    dma = pltpu.SemaphoreType.DMA
    blocked = pltpu.VMEM((2, blocks, channels * SUB, 128), BF16)
    edge = pltpu.VMEM((blocks // 2, channels * SUB, 128), BF16)
    smoothed, totals, tail = pl.pallas_call(
        functools.partial(kernel, nx, ny),
        out_shape=(
            pltpu.VMEM((channels, rows, cols), BF16),
            pltpu.VMEM((2 * channels, 128), F32),
            pltpu.VMEM((8, 128), F32),
        ),
        in_specs=[hbm_spec] * 5,
        out_specs=(vmem_spec, vmem_spec, vmem_spec),
        scratch_shapes=[
            pltpu.VMEM((channels, rows, cols), BF16),
            pltpu.VMEM((channels, rows, cols), BF16),
            pltpu.VMEM((rows, cols), F32),
            pltpu.VMEM((rows, cols), jnp.int32),
            pltpu.SMEM((channels,), F32),
            pltpu.VMEM((channels, SUB, 128), F32),
            pltpu.VMEM((rows, cols), F32),
            pltpu.VMEM((rows, cols), F32),
            blocked,
            blocked,
            blocked,
            edge,
            edge,
            edge,
            edge,
            pltpu.VMEM((2, channels, 2 * rows, 128), BF16),
            blocked,
            pltpu.VMEM((2, 2 * cols, 128), BF16),
            pltpu.VMEM((2, 2 * cols, 128), BF16),
            pltpu.VMEM((2, rows, 128), BF16),
            pltpu.VMEM((channels * SUB, 32 * SUB), F32),
            pltpu.VMEM((channels * SUB, 32 * SUB), F32),
            pltpu.VMEM((channels, 128), F32),
            pltpu.VMEM((channels, 128), F32),
            pltpu.VMEM((channels, 128), F32),
            pltpu.VMEM((channels * SUB, cols), F32),
            pltpu.VMEM((2 * pieces, 8, 128), F32),
            pltpu.VMEM((nx, own, 8, 128), F32),
            pltpu.VMEM((own, 8, 128), F32),
            pltpu.VMEM((ny, own, 8, 128), F32),
            pltpu.VMEM((own, 8, 128), F32),
            pltpu.VMEM((2 * pieces, 8, 128), F32),
            pltpu.VMEM((8, 128), F32),
            pltpu.VMEM((nx, 8, 128), F32),
            pltpu.VMEM((8, 128), F32),
            pltpu.VMEM((ny, 8, 128), F32),
            dma((3,)),
            dma((4,)),
            dma((n_chunks,)),
        ]
        + [dma((n_chunks,))] * 8
        + [dma((5,)), dma((5,))],
        compiler_params=pltpu.CompilerParams(
            collective_id=0, has_side_effects=True, vmem_limit_bytes=42 * 1024 * 1024
        ),
        cost_estimate=pl.CostEstimate(flops=5 * 10**9, bytes_accessed=13 * 2**20, transcendentals=0),
    )(*map(in_hbm, (instruments, regressors, outcome, land_mask, coefficients)))
    smoothed, hac_cov, new_coefficients = pl.pallas_call(
        finish,
        out_shape=(
            jax.ShapeDtypeStruct((channels, rows, cols), BF16),
            jax.ShapeDtypeStruct((channels, channels), F32),
            jax.ShapeDtypeStruct((1, channels), F32),
        ),
        in_specs=[vmem_spec] * 5,
        out_specs=(any_spec, vmem_spec, vmem_spec),
        scratch_shapes=[dma((4,))],
        compiler_params=pltpu.CompilerParams(vmem_limit_bytes=4 * 1024 * 1024),
        cost_estimate=pl.CostEstimate(flops=10**6, bytes_accessed=8 * 2**20, transcendentals=0),
    )(in_vmem(smoothed), in_vmem(totals), in_vmem(tail), coefficients.reshape(1, channels), weighting)
    return smoothed, hac_cov, new_coefficients.reshape(channels)


def solution(mesh):
    placed = (P(None, "gx", "gy"), P(None, "gx", "gy"), P("gx", "gy"), P("gx", "gy"), P(), P())
    return jax.shard_map(
        functools.partial(local, mesh.shape["gx"], mesh.shape["gy"]),
        mesh=mesh,
        in_specs=placed,
        out_specs=(P(None, "gx", "gy"), P(), P()),
        check_vma=False,
    )
```

```python
import functools

import jax
import jax.numpy as jnp
from jax import lax
from jax.experimental import pallas as pl
from jax.experimental.pallas import tpu as pltpu
from jax.sharding import PartitionSpec as P

B = 64
step_rate = 0.05
MESH = pl.DeviceIdType.MESH
F32 = jnp.float32
BF16 = jnp.bfloat16
CH = 8
SUB = 8
DEEP = 4
LAG = 1
COV_BLOCKS = ((0, 32), (32, 16), (48, 16))
JAC_BLOCK = 32
TAIL = 32


def iota(shape, dim):
    return lax.broadcasted_iota(jnp.int32, shape, dim)


def dot(a, b):
    return lax.dot_general(a, b, (((1,), (0,)), ((), ())), preferred_element_type=F32)


def dot_t(a, b):
    return lax.dot_general(a, b, (((1,), (1,)), ((), ())), preferred_element_type=F32)


def wide(ref, *at):
    return jnp.concatenate([ref[(0, *at)], ref[(1, *at)]], axis=-1)


def put_wide(ref, value):
    ref[0] = value[:, :128]
    ref[1] = value[:, 128:]


def hat(distance):
    return jnp.maximum(B + 1 - jnp.abs(distance), 0).astype(F32).astype(BF16)


def kernel(
    nx,
    ny,
    inst_h,
    reg_h,
    outcome_h,
    land_h,
    coef_h,
    sm,
    total_v,
    tail_v,
    inst,
    reg,
    outcome,
    land,
    coef_s,
    coefs,
    weighted,
    land_float,
    mom,
    inst_b,
    reg_b,
    send_l,
    send_r,
    y_l,
    y_r,
    rows_sm,
    sm_b,
    w_top,
    w_bot,
    w_col,
    acc_cov,
    acc_jac,
    cov,
    cov_tail,
    jac,
    sums,
    part,
    got1,
    sum1,
    got2,
    sum2,
    got3,
    tile,
    got4,
    sum4,
    got5,
    in_sem,
    reg_sem,
    inst_sem,
    yl_send,
    yl_recv,
    yr_send,
    yr_recv,
    zt_send,
    zt_recv,
    zb_send,
    zb_recv,
    ar_send,
    ar_recv,
):
    gx = lax.axis_index("gx")
    gy = lax.axis_index("gy")
    channels, rows, cols = inst.shape
    half = rows // 2
    n_chunks = channels // CH
    reg_rows = rows // 4
    blocks = rows // SUB

    def outcome_copy():
        return pltpu.make_async_copy(outcome_h, outcome, in_sem.at[0])

    def land_copy():
        return pltpu.make_async_copy(land_h, land, in_sem.at[1])

    def coef_copy():
        return pltpu.make_async_copy(coef_h, coef_s, in_sem.at[2])

    def reg_copy(r):
        at = pl.ds(pl.multiple_of(r * reg_rows, reg_rows), reg_rows)
        return pltpu.make_async_copy(reg_h.at[:, at, :], reg.at[:, at, :], reg_sem.at[r])

    def inst_copy(c):
        at = pl.ds(c * CH, CH)
        return pltpu.make_async_copy(inst_h.at[at], inst.at[at], inst_sem.at[c])

    coef_copy().start()
    reg_copy(0).start()
    outcome_copy().start()
    land_copy().start()
    for r in range(1, 4):
        reg_copy(r).start()
    for c in range(n_chunks):
        inst_copy(c).start()

    barrier = pltpu.get_barrier_semaphore()

    def greet_x(o, carry):
        pl.semaphore_signal(barrier, inc=1, device_id=((gx + o) % nx, gy), device_id_type=MESH)
        return carry

    def greet_y(o, carry):
        pl.semaphore_signal(barrier, inc=1, device_id=(gx, (gy + o) % ny), device_id_type=MESH)
        return carry

    lax.fori_loop(1, nx, greet_x, 0)
    lax.fori_loop(1, ny, greet_y, 0)

    src = iota((cols, cols), 0)
    dst = iota((cols, cols), 1)
    own_band = hat(src - dst)
    low = src % half
    side = jnp.where(src < 2 * half, low - half, low + cols)
    ramp = jnp.maximum(B + 1 - jnp.abs(side - dst), 0).astype(F32)
    is_top = (src // half) % 2 == 0
    put_wide(w_top, jnp.concatenate([own_band, jnp.where(is_top, ramp, 0.0).astype(BF16)], axis=0))
    put_wide(w_bot, jnp.concatenate([own_band, jnp.where(is_top, 0.0, ramp).astype(BF16)], axis=0))
    put_wide(w_col, hat(iota((rows, 2 * rows), 1) - half - iota((rows, 2 * rows), 0)))

    @pl.when(gy == 0)
    def _():
        y_l[...] = jnp.zeros_like(y_l)

    @pl.when(gy == ny - 1)
    def _():
        y_r[...] = jnp.zeros_like(y_r)

    def clear(start):
        def body(k, carry):
            rows_sm[:, k, start : start + half, :] = jnp.zeros((2, half, 128), BF16)
            return carry

        lax.fori_loop(0, channels, body, 0)

    @pl.when(gx == 0)
    def _():
        clear(0)

    @pl.when(gx == nx - 1)
    def _():
        clear(rows + half)

    cov[...] = jnp.zeros_like(cov)
    cov_tail[...] = jnp.zeros_like(cov_tail)
    jac[...] = jnp.zeros_like(jac)
    acc_cov[...] = jnp.zeros_like(acc_cov)
    acc_jac[...] = jnp.zeros_like(acc_jac)

    coef_copy().wait()
    for p in range(channels):
        coefs[p] = jnp.full((SUB, 128), coef_s[p], F32)
    coefs[...] = coefs[...].astype(BF16).astype(F32)

    def residuals(r, carry):
        reg_copy(r).wait()
        at = pl.ds(pl.multiple_of(r * reg_rows, reg_rows), reg_rows)

        def add(q, total):
            for u in range(8):
                p = q * 8 + u
                one = jnp.concatenate([coefs[p]] * (cols // 128), axis=1)
                total = total + reg[p, at, :].astype(F32) * jnp.concatenate([one] * (reg_rows // SUB), axis=0)
            return total

        fitted = lax.fori_loop(0, channels // 8, add, jnp.zeros((reg_rows, cols), F32))

        @pl.when(r == 0)
        def _():
            outcome_copy().wait()
            land_copy().wait()

        here = land[at, :].astype(F32)
        weighted[at, :] = here * (outcome[at, :] - fitted)
        land_float[at, :] = here
        return carry

    lax.fori_loop(0, 4, residuals, 0)

    def chunk_rows(c):
        return pl.ds(pl.multiple_of(c * CH * SUB, CH * SUB), CH * SUB)

    def to_left(c):
        return pltpu.make_async_remote_copy(
            src_ref=send_l.at[:, chunk_rows(c), :],
            dst_ref=y_r.at[:, chunk_rows(c), :],
            send_sem=yl_send.at[c],
            recv_sem=yr_recv.at[c],
            device_id=(gx, gy - 1),
            device_id_type=MESH,
        )

    def to_right(c):
        return pltpu.make_async_remote_copy(
            src_ref=send_r.at[:, chunk_rows(c), :],
            dst_ref=y_l.at[:, chunk_rows(c), :],
            send_sem=yr_send.at[c],
            recv_sem=yl_recv.at[c],
            device_id=(gx, gy + 1),
            device_id_type=MESH,
        )

    def to_upper(c):
        at = pl.ds(c * CH, CH)
        return pltpu.make_async_remote_copy(
            src_ref=rows_sm.at[:, at, half : 2 * half, :],
            dst_ref=rows_sm.at[:, at, 3 * half : 4 * half, :],
            send_sem=zt_send.at[c],
            recv_sem=zb_recv.at[c],
            device_id=(gx - 1, gy),
            device_id_type=MESH,
        )

    def to_lower(c):
        at = pl.ds(c * CH, CH)
        return pltpu.make_async_remote_copy(
            src_ref=rows_sm.at[:, at, 2 * half : 3 * half, :],
            dst_ref=rows_sm.at[:, at, 0:half, :],
            send_sem=zb_send.at[c],
            recv_sem=zt_recv.at[c],
            device_id=(gx + 1, gy),
            device_id_type=MESH,
        )

    has_left, has_right = gy > 0, gy < ny - 1
    has_upper, has_lower = gx > 0, gx < nx - 1

    def send_edges(c):
        @pl.when(has_left)
        def _():
            to_left(c).start()

        @pl.when(has_right)
        def _():
            to_right(c).start()

    first_lanes = iota((2 * SUB, 128), 1) < B

    def store_blocked(ref, first_block, at, one, two):
        ref[first_block, at, :] = jnp.concatenate([one[:SUB], two[:SUB]], axis=0).astype(BF16)
        ref[first_block + 1, at, :] = jnp.concatenate([one[SUB:], two[SUB:]], axis=0).astype(BF16)

    def store_wide(ref, first_block, at, one, two):
        for h in range(2):
            lanes = slice(128 * h, 128 * h + 128)
            store_blocked(ref.at[h], first_block, at, one[:, lanes], two[:, lanes])

    def moments(c, carry):
        inst_copy(c).wait()

        def channel_pair(u, inner):
            k = c * CH + 2 * u
            at = pl.ds(pl.multiple_of(k * SUB, 2 * SUB), 2 * SUB)
            for r in range(0, half, 2 * SUB):
                first = r // SUB
                upper, lower = slice(r, r + 2 * SUB), slice(half + r, half + r + 2 * SUB)
                w_upper, w_lower = weighted[upper, :], weighted[lower, :]
                raw = [(inst[k + v, upper, :].astype(F32), inst[k + v, lower, :].astype(F32)) for v in range(2)]
                prods = [(top * w_upper, bot * w_lower) for top, bot in raw]
                store_wide(inst_b, first, at, raw[0][0], raw[1][0])
                store_wide(inst_b, blocks // 2 + first, at, raw[0][1], raw[1][1])
                store_wide(mom, first, at, prods[0][0], prods[1][0])
                store_wide(mom, blocks // 2 + first, at, prods[0][1], prods[1][1])
                left = [
                    jnp.where(first_lanes, top[:, :128], pltpu.roll(bot[:, :128], B, 1)) for top, bot in prods
                ]
                right = [
                    jnp.where(first_lanes, pltpu.roll(top[:, cols - 128 :], B, 1), bot[:, cols - 128 :])
                    for top, bot in prods
                ]
                store_blocked(send_l, first, at, left[0], left[1])
                store_blocked(send_r, first, at, right[0], right[1])
            return inner

        lax.fori_loop(0, CH // 2, channel_pair, 0)

        @pl.when(c == 0)
        def _():
            pl.semaphore_wait(barrier, nx - 1 + ny - 1)

        send_edges(c)
        return carry

    lax.fori_loop(0, n_chunks, moments, 0)

    def block_regressors(u, carry):
        at = pl.ds(pl.multiple_of(2 * u * SUB, 2 * SUB), 2 * SUB)
        for r in range(0, rows, 2 * SUB):
            here = land_float[r : r + 2 * SUB, :]
            one = reg[2 * u, r : r + 2 * SUB, :].astype(F32) * here
            two = reg[2 * u + 1, r : r + 2 * SUB, :].astype(F32) * here
            store_wide(reg_b, r // SUB, at, one, two)
        return carry

    def product(acc, left_ref, left_rows, right_ref, right_rows, b):
        at = (slice(0, left_rows.size), slice(0, right_rows.size))
        lhs = jnp.concatenate([wide(left_ref, b + u, left_rows) for u in range(DEEP)], axis=1)
        rhs = jnp.concatenate([wide(right_ref, b + u, right_rows) for u in range(DEEP)], axis=1)
        acc[at] += dot_t(lhs, rhs)

    def fold(acc, left_count, right_count, first_column):
        at = (slice(0, left_count * SUB), slice(0, right_count * SUB))
        shape = (1, SUB, right_count * SUB)
        kept = jnp.where(iota(shape, 2) % SUB == iota(shape, 1), acc[at].reshape(left_count, SUB, right_count * SUB), 0.0)
        kept = jnp.sum(kept, axis=1)
        pick = iota((right_count * SUB, 128), 0) // SUB + first_column == iota((right_count * SUB, 128), 1)
        acc[...] = jnp.zeros_like(acc)
        return lax.dot_general(
            kept,
            pick.astype(F32),
            (((1,), (0,)), ((), ())),
            precision=lax.Precision.HIGHEST,
            preferred_element_type=F32,
        )

    def jac_part(first, b):
        at = pl.ds(pl.multiple_of(first * SUB, JAC_BLOCK * SUB), JAC_BLOCK * SUB)
        product(acc_jac, inst_b, pl.ds(0, channels * SUB), reg_b, at, b)

    def jac_fold(first):
        jac[...] += fold(acc_jac, channels, JAC_BLOCK, first)

    def cov_part(first, count, b):
        left = pl.ds(first * SUB, (channels - first) * SUB)
        product(acc_cov, mom, left, sm_b, pl.ds(first * SUB, count * SUB), b)

    def cov_fold(ref, first, count):
        ref[first:, :] += fold(acc_cov, channels - first, count, first)

    def moment_sums(b):
        if b == 0:
            sums[...] = jnp.zeros_like(sums)
        sums[...] += wide(mom, b).astype(F32) + wide(mom, b + 1).astype(F32)

    def smooth_rows(c):
        @pl.when(has_left)
        def _():
            to_right(c).wait_recv()

        @pl.when(has_right)
        def _():
            to_left(c).wait_recv()

        at = chunk_rows(c)
        for start, weights in ((0, w_top), (half, w_bot)):
            lhs = jnp.concatenate(
                [
                    jnp.concatenate([wide(mom, start // SUB + b, at), y_l[b, at, :], y_r[b, at, :]], axis=1)
                    for b in range(half // SUB)
                ],
                axis=0,
            )
            total = dot(lhs, wide(weights)) * (1.0 / (B + 1))
            for b in range(0, half // SUB, 2):
                for u in range(CH):
                    one = total[(b * CH + u) * SUB : (b * CH + u + 1) * SUB]
                    two = total[((b + 1) * CH + u) * SUB : ((b + 1) * CH + u + 1) * SUB]
                    place = half + start + b * SUB
                    both = jnp.concatenate([one, two], axis=0).astype(BF16)
                    rows_sm[0, c * CH + u, place : place + 2 * SUB, :] = both[:, :128]
                    rows_sm[1, c * CH + u, place : place + 2 * SUB, :] = both[:, 128:]

        @pl.when(has_upper)
        def _():
            to_upper(c).start()

        @pl.when(has_lower)
        def _():
            to_lower(c).start()

    def land_columns(c):
        @pl.when(has_upper)
        def _():
            to_lower(c).wait_recv()

        @pl.when(has_lower)
        def _():
            to_upper(c).wait_recv()

    def smooth_columns(c):
        for u in range(0, CH, 2):
            k = c * CH + u
            pair = [dot(wide(w_col), wide(rows_sm, k + v)) * (1.0 / (B + 1) ** 2) for v in range(2)]
            sm[k] = pair[0].astype(BF16)
            sm[k + 1] = pair[1].astype(BF16)
            at = pl.ds(pl.multiple_of(k * SUB, 2 * SUB), 2 * SUB)
            for r in range(0, rows, 2 * SUB):
                store_wide(sm_b, r // SUB, at, pair[0][r : r + 2 * SUB], pair[1][r : r + 2 * SUB])

    pieces = channels // 8
    own_pieces = 2 * pieces // nx

    def send_all(number, peers, me, copy):
        def send(o, carry):
            copy(number, (me + o) % peers).start()
            return carry

        lax.fori_loop(1, peers, send, 0)

    def land_all(number, landed):
        pltpu.make_async_copy(landed, landed, ar_recv.at[number]).wait()
        pltpu.make_async_copy(landed, landed, ar_send.at[number]).wait()

    def own(g):
        return pl.ds(g * own_pieces, own_pieces)

    def remote(number, src, dst, device):
        return pltpu.make_async_remote_copy(
            src_ref=src,
            dst_ref=dst,
            send_sem=ar_send.at[number],
            recv_sem=ar_recv.at[number],
            device_id=device,
            device_id_type=MESH,
        )

    def scatter(number, g):
        return remote(number, part.at[own(g)], got1.at[gx], (g, gy))

    def across(number, g):
        return remote(number, sum1, got2.at[gy], (gx, g))

    def gather(number, g):
        return remote(number, sum2, got3.at[own(gx)], (g, gy))

    def tail_x(number, g):
        return remote(number, tile, got4.at[gx], (g, gy))

    def tail_y(number, g):
        return remote(number, sum4, got5.at[gy], (gx, g))

    def early_scatter():
        count = jnp.sum(jnp.sum(land_float[...], axis=0, keepdims=True), axis=1, keepdims=True)
        columns = jnp.sum(jnp.sum(sums[...].reshape(channels, SUB, cols), axis=1), axis=1, keepdims=True)
        right_half = iota((channels, 128), 1) >= channels
        as_row = jnp.sum(
            jnp.where(iota((channels, 128), 1) - channels == iota((channels, 128), 0), columns, 0.0),
            axis=0,
            keepdims=True,
        )
        part[0:pieces] = jnp.where(right_half, count, cov[...]).reshape(pieces, 8, 128)
        part[pieces : 2 * pieces] = jnp.where(right_half, as_row, jac[...]).reshape(pieces, 8, 128)
        got1[gx] = part[own(gx)]
        send_all(0, nx, gx, scatter)

    def early_across():
        land_all(0, got1.at[0 : nx - 1])
        sum1[...] = jnp.sum(got1[...], axis=0)
        got2[gy] = sum1[...]
        send_all(1, ny, gy, across)

    def early_gather():
        land_all(1, got2.at[0 : ny - 1])
        sum2[...] = jnp.sum(got2[...], axis=0)
        got3[own(gx)] = sum2[...]
        send_all(2, nx, gx, gather)

    last = n_chunks + LAG - 1

    def pipeline(t, carry):
        @pl.when(t < n_chunks)
        def _():
            smooth_rows(t)

        @pl.when(t == 0)
        def _():
            lax.fori_loop(0, channels // 2, block_regressors, 0)
            for b in range(0, blocks, 2):
                moment_sums(b)

        @pl.when(t >= LAG)
        def _():
            land_columns(t - LAG)

        @pl.when(jnp.logical_and(t >= 1, t <= 4))
        def _():
            for u in range(0, blocks // 2, DEEP):
                jac_part((t - 1) // 2 * JAC_BLOCK, (t - 1) % 2 * (blocks // 2) + u)
            smooth_columns(t - LAG)

        for g in range(channels // JAC_BLOCK):

            @pl.when(t == 2 + 2 * g)
            def _(g=g):
                jac_fold(g * JAC_BLOCK)

        first, count = COV_BLOCKS[0]
        begin = (first + count) // CH + LAG

        @pl.when(jnp.logical_or(t == begin, t == begin + 1))
        def _(first=first, count=count, begin=begin):
            for u in range(0, blocks // 2, DEEP):
                cov_part(first, count, (t - begin) * (blocks // 2) + u)
            smooth_columns(t - LAG)

        @pl.when(t == begin + 1)
        def _(first=first, count=count):
            cov_fold(cov, first, count)
            early_scatter()

        first, count = COV_BLOCKS[1]
        begin = (first + count) // CH + LAG

        @pl.when(t == begin)
        def _(first=first, count=count):
            early_across()
            for b in range(0, blocks, DEEP):
                cov_part(first, count, b)
            smooth_columns(t - LAG)
            cov_fold(cov_tail, first, count)

        @pl.when(t == last)
        def _():
            early_gather()
            smooth_columns(t - LAG)

        return carry

    lax.fori_loop(0, last + 1, pipeline, 0)

    first, count = COV_BLOCKS[2]
    for b in range(0, blocks, DEEP):
        cov_part(first, count, b)
    cov_fold(cov_tail, first, count)

    lane_group = iota((8, 128), 1) // 32
    packed = jnp.zeros((8, 128), F32)
    for g in range((channels - TAIL) // 8):
        piece = cov_tail[TAIL + 8 * g : TAIL + 8 * g + 8, :]
        packed = jnp.where(lane_group == g, pltpu.roll(piece, (32 * g - TAIL) % 128, 1), packed)
    tile[...] = packed
    send_all(3, nx, gx, tail_x)
    got4[gx] = tile[...]

    def drain(c, carry):
        @pl.when(has_left)
        def _():
            to_left(c).wait_send()

        @pl.when(has_right)
        def _():
            to_right(c).wait_send()

        @pl.when(has_upper)
        def _():
            to_upper(c).wait_send()

        @pl.when(has_lower)
        def _():
            to_lower(c).wait_send()

        return carry

    lax.fori_loop(0, n_chunks, drain, 0)
    land_all(2, got3.at[0 : (nx - 1) * own_pieces])
    total_v[...] = got3[...].reshape(2 * channels, 128)

    land_all(3, got4.at[0 : nx - 1])
    sum4[...] = jnp.sum(got4[...], axis=0)
    send_all(4, ny, gy, tail_y)
    got5[gy] = sum4[...]
    land_all(4, got5.at[0 : ny - 1])
    tail_v[...] = jnp.sum(got5[...], axis=0)


def finish(s_in, total_v, tail_v, coef_v, wgt_v, s_out, hac_v, new_v, sem):
    channels = s_in.shape[0]
    share = channels // 4

    def move(c):
        at = pl.ds(c * share, share)
        return pltpu.make_async_copy(s_in.at[at], s_out.at[at], sem.at[c])

    for c in range(4):
        move(c).start()
    first, second = total_v[0:channels, :], total_v[channels : 2 * channels, :]
    land_total = first[:, channels : channels + 1]
    tail = jnp.concatenate([pltpu.roll(tail_v[...], (TAIL - 32 * g) % 128, 1) for g in range((channels - TAIL) // 8)], axis=0)
    bottom = jnp.where(iota(tail.shape, 1) >= TAIL, tail, first[TAIL:, :])
    lower = jnp.concatenate([first[:TAIL, :], bottom], axis=0)[:, :channels]
    row, column = iota((channels, channels), 0), iota((channels, channels), 1)
    held = row >= 0
    for start, count in COV_BLOCKS:
        held = jnp.logical_and(held, jnp.logical_or(column < start, row >= start))
    hac_v[...] = jnp.where(held, lower, lower.T) * ((B + 1) / land_total)
    mean = second[0:1, channels:] / land_total[0:1, :]
    weighed = jnp.sum(wgt_v[...] * mean, axis=1, keepdims=True)
    jacobian = -second[:, :channels] / land_total
    gradient = 2.0 * jnp.sum(jacobian * weighed, axis=0, keepdims=True)
    new_v[...] = coef_v[...] - step_rate * gradient
    for c in range(4):
        move(c).wait()


def local(nx, ny, instruments, regressors, outcome, land_mask, coefficients, weighting):
    channels, rows, cols = instruments.shape
    n_chunks = channels // CH
    pieces = channels // 8
    own = 2 * pieces // nx
    blocks = rows // SUB
    any_spec = pl.BlockSpec(memory_space=pl.ANY)
    in_hbm = functools.partial(pltpu.with_memory_space_constraint, memory_space=pltpu.HBM)
    in_vmem = functools.partial(pltpu.with_memory_space_constraint, memory_space=pltpu.VMEM)
    hbm_spec = pl.BlockSpec(memory_space=pltpu.HBM)
    vmem_spec = pl.BlockSpec(memory_space=pltpu.VMEM)
    dma = pltpu.SemaphoreType.DMA
    blocked = pltpu.VMEM((2, blocks, channels * SUB, 128), BF16)
    edge = pltpu.VMEM((blocks // 2, channels * SUB, 128), BF16)
    smoothed, totals, tail = pl.pallas_call(
        functools.partial(kernel, nx, ny),
        out_shape=(
            pltpu.VMEM((channels, rows, cols), BF16),
            pltpu.VMEM((2 * channels, 128), F32),
            pltpu.VMEM((8, 128), F32),
        ),
        in_specs=[hbm_spec] * 5,
        out_specs=(vmem_spec, vmem_spec, vmem_spec),
        scratch_shapes=[
            pltpu.VMEM((channels, rows, cols), BF16),
            pltpu.VMEM((channels, rows, cols), BF16),
            pltpu.VMEM((rows, cols), F32),
            pltpu.VMEM((rows, cols), jnp.int32),
            pltpu.SMEM((channels,), F32),
            pltpu.VMEM((channels, SUB, 128), F32),
            pltpu.VMEM((rows, cols), F32),
            pltpu.VMEM((rows, cols), F32),
            blocked,
            blocked,
            blocked,
            edge,
            edge,
            edge,
            edge,
            pltpu.VMEM((2, channels, 2 * rows, 128), BF16),
            blocked,
            pltpu.VMEM((2, 2 * cols, 128), BF16),
            pltpu.VMEM((2, 2 * cols, 128), BF16),
            pltpu.VMEM((2, rows, 128), BF16),
            pltpu.VMEM((channels * SUB, 32 * SUB), F32),
            pltpu.VMEM((channels * SUB, 32 * SUB), F32),
            pltpu.VMEM((channels, 128), F32),
            pltpu.VMEM((channels, 128), F32),
            pltpu.VMEM((channels, 128), F32),
            pltpu.VMEM((channels * SUB, cols), F32),
            pltpu.VMEM((2 * pieces, 8, 128), F32),
            pltpu.VMEM((nx, own, 8, 128), F32),
            pltpu.VMEM((own, 8, 128), F32),
            pltpu.VMEM((ny, own, 8, 128), F32),
            pltpu.VMEM((own, 8, 128), F32),
            pltpu.VMEM((2 * pieces, 8, 128), F32),
            pltpu.VMEM((8, 128), F32),
            pltpu.VMEM((nx, 8, 128), F32),
            pltpu.VMEM((8, 128), F32),
            pltpu.VMEM((ny, 8, 128), F32),
            dma((3,)),
            dma((4,)),
            dma((n_chunks,)),
        ]
        + [dma((n_chunks,))] * 8
        + [dma((5,)), dma((5,))],
        compiler_params=pltpu.CompilerParams(
            collective_id=0, has_side_effects=True, vmem_limit_bytes=42 * 1024 * 1024
        ),
        cost_estimate=pl.CostEstimate(flops=5 * 10**9, bytes_accessed=13 * 2**20, transcendentals=0),
    )(*map(in_hbm, (instruments, regressors, outcome, land_mask, coefficients)))
    smoothed, hac_cov, new_coefficients = pl.pallas_call(
        finish,
        out_shape=(
            jax.ShapeDtypeStruct((channels, rows, cols), BF16),
            jax.ShapeDtypeStruct((channels, channels), F32),
            jax.ShapeDtypeStruct((1, channels), F32),
        ),
        in_specs=[vmem_spec] * 5,
        out_specs=(any_spec, vmem_spec, vmem_spec),
        scratch_shapes=[dma((4,))],
        compiler_params=pltpu.CompilerParams(vmem_limit_bytes=4 * 1024 * 1024),
        cost_estimate=pl.CostEstimate(flops=10**6, bytes_accessed=8 * 2**20, transcendentals=0),
    )(in_vmem(smoothed), in_vmem(totals), in_vmem(tail), coefficients.reshape(1, channels), weighting)
    return smoothed, hac_cov, new_coefficients.reshape(channels)


def solution(mesh):
    placed = (P(None, "gx", "gy"), P(None, "gx", "gy"), P("gx", "gy"), P("gx", "gy"), P(), P())
    return jax.shard_map(
        functools.partial(local, mesh.shape["gx"], mesh.shape["gy"]),
        mesh=mesh,
        in_specs=placed,
        out_specs=(P(None, "gx", "gy"), P(), P()),
        check_vma=False,
    )
```

```python
import functools

import jax
import jax.numpy as jnp
from jax import lax
from jax.experimental import pallas as pl
from jax.experimental.pallas import tpu as pltpu
from jax.sharding import PartitionSpec as P

B = 64
step_rate = 0.05
MESH = pl.DeviceIdType.MESH
F32 = jnp.float32
BF16 = jnp.bfloat16
CH = 8
SUB = 8
LAG = 1
COV_BLOCKS = ((0, 32), (32, 16), (48, 16))
JAC_BLOCK = 32
TAIL = 32


def iota(shape, dim):
    return lax.broadcasted_iota(jnp.int32, shape, dim)


def dot(a, b):
    return lax.dot_general(a, b, (((1,), (0,)), ((), ())), preferred_element_type=F32)


def dot_t(a, b):
    return lax.dot_general(a, b, (((1,), (1,)), ((), ())), preferred_element_type=F32)


def wide(ref, *at):
    return jnp.concatenate([ref[(0, *at)], ref[(1, *at)]], axis=-1)


def put_wide(ref, value):
    ref[0] = value[:, :128]
    ref[1] = value[:, 128:]


def hat(distance):
    return jnp.maximum(B + 1 - jnp.abs(distance), 0).astype(F32).astype(BF16)


def kernel(
    nx,
    ny,
    inst_h,
    reg_h,
    outcome_h,
    land_h,
    coef_h,
    sm,
    total_v,
    tail_v,
    inst,
    reg,
    outcome,
    land,
    coef_s,
    coefs,
    weighted,
    land_float,
    mom,
    inst_b,
    reg_b,
    send_l,
    send_r,
    y_l,
    y_r,
    rows_sm,
    sm_b,
    w_own,
    w_edge,
    w_col,
    edges,
    acc_cov,
    acc_jac,
    cov,
    cov_tail,
    jac,
    sums,
    part,
    got1,
    sum1,
    got2,
    sum2,
    got3,
    tile,
    got4,
    sum4,
    got5,
    in_sem,
    reg_sem,
    inst_sem,
    yl_send,
    yl_recv,
    yr_send,
    yr_recv,
    zt_send,
    zt_recv,
    zb_send,
    zb_recv,
    ar_send,
    ar_recv,
):
    gx = lax.axis_index("gx")
    gy = lax.axis_index("gy")
    channels, rows, cols = inst.shape
    half = rows // 2
    n_chunks = channels // CH
    reg_rows = rows // 4
    blocks = rows // SUB

    def outcome_copy():
        return pltpu.make_async_copy(outcome_h, outcome, in_sem.at[0])

    def land_copy():
        return pltpu.make_async_copy(land_h, land, in_sem.at[1])

    def coef_copy():
        return pltpu.make_async_copy(coef_h, coef_s, in_sem.at[2])

    def reg_copy(r):
        at = pl.ds(pl.multiple_of(r * reg_rows, reg_rows), reg_rows)
        return pltpu.make_async_copy(reg_h.at[:, at, :], reg.at[:, at, :], reg_sem.at[r])

    def inst_copy(c):
        at = pl.ds(c * CH, CH)
        return pltpu.make_async_copy(inst_h.at[at], inst.at[at], inst_sem.at[c])

    coef_copy().start()
    reg_copy(0).start()
    outcome_copy().start()
    land_copy().start()
    for r in range(1, 4):
        reg_copy(r).start()
    for c in range(n_chunks):
        inst_copy(c).start()

    barrier = pltpu.get_barrier_semaphore()

    def greet_x(o, carry):
        pl.semaphore_signal(barrier, inc=1, device_id=((gx + o) % nx, gy), device_id_type=MESH)
        return carry

    def greet_y(o, carry):
        pl.semaphore_signal(barrier, inc=1, device_id=(gx, (gy + o) % ny), device_id_type=MESH)
        return carry

    lax.fori_loop(1, nx, greet_x, 0)
    lax.fori_loop(1, ny, greet_y, 0)

    src = iota((cols, cols), 0)
    dst = iota((cols, cols), 1)
    put_wide(w_own, hat(src - dst))
    lane = jnp.bitwise_and(dst, 127)
    column = jnp.where(lane < B, lane, lane + cols - 128)
    low = jnp.bitwise_and(src, B - 1)
    side = jnp.where(src < 2 * B, low - B, low + cols)
    same_half = (jnp.bitwise_and(src, B) == 0) == (dst < 128)
    put_wide(w_edge, jnp.where(same_half, jnp.maximum(B + 1 - jnp.abs(side - column), 0), 0).astype(F32).astype(BF16))
    put_wide(w_col, hat(iota((rows, 2 * rows), 1) - half - iota((rows, 2 * rows), 0)))

    @pl.when(gy == 0)
    def _():
        y_l[...] = jnp.zeros_like(y_l)

    @pl.when(gy == ny - 1)
    def _():
        y_r[...] = jnp.zeros_like(y_r)

    def clear(start):
        def body(k, carry):
            rows_sm[:, k, start : start + half, :] = jnp.zeros((2, half, 128), BF16)
            return carry

        lax.fori_loop(0, channels, body, 0)

    @pl.when(gx == 0)
    def _():
        clear(0)

    @pl.when(gx == nx - 1)
    def _():
        clear(rows + half)

    cov[...] = jnp.zeros_like(cov)
    cov_tail[...] = jnp.zeros_like(cov_tail)
    jac[...] = jnp.zeros_like(jac)
    acc_cov[...] = jnp.zeros_like(acc_cov)
    acc_jac[...] = jnp.zeros_like(acc_jac)

    coef_copy().wait()
    for p in range(channels):
        coefs[p] = jnp.full((SUB, 128), coef_s[p], F32)
    coefs[...] = coefs[...].astype(BF16).astype(F32)

    def residuals(r, carry):
        reg_copy(r).wait()
        at = pl.ds(pl.multiple_of(r * reg_rows, reg_rows), reg_rows)

        def add(q, total):
            for u in range(8):
                p = q * 8 + u
                one = jnp.concatenate([coefs[p]] * (cols // 128), axis=1)
                total = total + reg[p, at, :].astype(F32) * jnp.concatenate([one] * (reg_rows // SUB), axis=0)
            return total

        fitted = lax.fori_loop(0, channels // 8, add, jnp.zeros((reg_rows, cols), F32))

        @pl.when(r == 0)
        def _():
            outcome_copy().wait()
            land_copy().wait()

        here = land[at, :].astype(F32)
        weighted[at, :] = here * (outcome[at, :] - fitted)
        land_float[at, :] = here
        return carry

    lax.fori_loop(0, 4, residuals, 0)

    def chunk_rows(c):
        return pl.ds(pl.multiple_of(c * CH * SUB, CH * SUB), CH * SUB)

    def to_left(c):
        return pltpu.make_async_remote_copy(
            src_ref=send_l.at[:, chunk_rows(c), :],
            dst_ref=y_r.at[:, chunk_rows(c), :],
            send_sem=yl_send.at[c],
            recv_sem=yr_recv.at[c],
            device_id=(gx, gy - 1),
            device_id_type=MESH,
        )

    def to_right(c):
        return pltpu.make_async_remote_copy(
            src_ref=send_r.at[:, chunk_rows(c), :],
            dst_ref=y_l.at[:, chunk_rows(c), :],
            send_sem=yr_send.at[c],
            recv_sem=yl_recv.at[c],
            device_id=(gx, gy + 1),
            device_id_type=MESH,
        )

    def to_upper(c):
        at = pl.ds(c * CH, CH)
        return pltpu.make_async_remote_copy(
            src_ref=rows_sm.at[:, at, half : 2 * half, :],
            dst_ref=rows_sm.at[:, at, 3 * half : 4 * half, :],
            send_sem=zt_send.at[c],
            recv_sem=zb_recv.at[c],
            device_id=(gx - 1, gy),
            device_id_type=MESH,
        )

    def to_lower(c):
        at = pl.ds(c * CH, CH)
        return pltpu.make_async_remote_copy(
            src_ref=rows_sm.at[:, at, 2 * half : 3 * half, :],
            dst_ref=rows_sm.at[:, at, 0:half, :],
            send_sem=zb_send.at[c],
            recv_sem=zt_recv.at[c],
            device_id=(gx + 1, gy),
            device_id_type=MESH,
        )

    has_left, has_right = gy > 0, gy < ny - 1
    has_upper, has_lower = gx > 0, gx < nx - 1

    def send_edges(c):
        @pl.when(has_left)
        def _():
            to_left(c).start()

        @pl.when(has_right)
        def _():
            to_right(c).start()

    first_lanes = iota((2 * SUB, 128), 1) < B

    def store_blocked(ref, first_block, at, one, two):
        ref[first_block, at, :] = jnp.concatenate([one[:SUB], two[:SUB]], axis=0).astype(BF16)
        ref[first_block + 1, at, :] = jnp.concatenate([one[SUB:], two[SUB:]], axis=0).astype(BF16)

    def store_wide(ref, first_block, at, one, two):
        for h in range(2):
            lanes = slice(128 * h, 128 * h + 128)
            store_blocked(ref.at[h], first_block, at, one[:, lanes], two[:, lanes])

    def moments(c, carry):
        inst_copy(c).wait()

        def channel_pair(u, inner):
            k = c * CH + 2 * u
            at = pl.ds(pl.multiple_of(k * SUB, 2 * SUB), 2 * SUB)
            for r in range(0, half, 2 * SUB):
                first = r // SUB
                upper, lower = slice(r, r + 2 * SUB), slice(half + r, half + r + 2 * SUB)
                w_upper, w_lower = weighted[upper, :], weighted[lower, :]
                raw = [(inst[k + v, upper, :].astype(F32), inst[k + v, lower, :].astype(F32)) for v in range(2)]
                prods = [(top * w_upper, bot * w_lower) for top, bot in raw]
                store_wide(inst_b, first, at, raw[0][0], raw[1][0])
                store_wide(inst_b, blocks // 2 + first, at, raw[0][1], raw[1][1])
                store_wide(mom, first, at, prods[0][0], prods[1][0])
                store_wide(mom, blocks // 2 + first, at, prods[0][1], prods[1][1])
                left = [
                    jnp.where(first_lanes, top[:, :128], pltpu.roll(bot[:, :128], B, 1)) for top, bot in prods
                ]
                right = [
                    jnp.where(first_lanes, pltpu.roll(top[:, cols - 128 :], B, 1), bot[:, cols - 128 :])
                    for top, bot in prods
                ]
                store_blocked(send_l, first, at, left[0], left[1])
                store_blocked(send_r, first, at, right[0], right[1])
            return inner

        lax.fori_loop(0, CH // 2, channel_pair, 0)

        @pl.when(c == 0)
        def _():
            pl.semaphore_wait(barrier, nx - 1 + ny - 1)

        send_edges(c)
        return carry

    lax.fori_loop(0, n_chunks, moments, 0)

    def block_regressors(u, carry):
        at = pl.ds(pl.multiple_of(2 * u * SUB, 2 * SUB), 2 * SUB)
        for r in range(0, rows, 2 * SUB):
            here = land_float[r : r + 2 * SUB, :]
            one = reg[2 * u, r : r + 2 * SUB, :].astype(F32) * here
            two = reg[2 * u + 1, r : r + 2 * SUB, :].astype(F32) * here
            store_wide(reg_b, r // SUB, at, one, two)
        return carry

    def product(acc, left_ref, left_rows, right_ref, right_rows, b):
        at = (slice(0, left_rows.size), slice(0, right_rows.size))
        for u in range(2):
            acc[at] += dot_t(wide(left_ref, b + u, left_rows), wide(right_ref, b + u, right_rows))

    def fold(acc, left_count, right_count, first_column):
        at = (slice(0, left_count * SUB), slice(0, right_count * SUB))
        shape = (1, SUB, right_count * SUB)
        kept = jnp.where(jnp.bitwise_and(iota(shape, 2), SUB - 1) == iota(shape, 1), acc[at].reshape(left_count, SUB, right_count * SUB), 0.0)
        kept = jnp.sum(kept, axis=1)
        from_pick = iota((right_count * SUB, 128), 0) - (iota((right_count * SUB, 128), 1) - first_column) * SUB
        pick = jnp.logical_and(from_pick >= 0, from_pick < SUB)
        acc[...] = jnp.zeros_like(acc)
        return lax.dot_general(
            kept,
            pick.astype(F32),
            (((1,), (0,)), ((), ())),
            precision=lax.Precision.HIGHEST,
            preferred_element_type=F32,
        )

    def jac_part(first, b):
        at = pl.ds(pl.multiple_of(first * SUB, JAC_BLOCK * SUB), JAC_BLOCK * SUB)
        product(acc_jac, inst_b, pl.ds(0, channels * SUB), reg_b, at, b)

    def jac_fold(first):
        jac[...] += fold(acc_jac, channels, JAC_BLOCK, first)

    def cov_part(first, count, b):
        left = pl.ds(first * SUB, (channels - first) * SUB)
        product(acc_cov, mom, left, sm_b, pl.ds(first * SUB, count * SUB), b)

    def cov_fold(ref, first, count):
        ref[first:, :] += fold(acc_cov, channels - first, count, first)

    def moment_sums(q, carry):
        at = pl.ds(pl.multiple_of(q * 64, 64), 64)
        total = wide(mom, 0, at).astype(F32)
        for b in range(1, blocks):
            total = total + wide(mom, b, at).astype(F32)
        sums[at, :] = total
        return carry

    def smooth_rows(c):
        @pl.when(has_left)
        def _():
            to_right(c).wait_recv()

        @pl.when(has_right)
        def _():
            to_left(c).wait_recv()

        at = chunk_rows(c)
        n_half = half // SUB
        outer = jnp.concatenate(
            [jnp.concatenate([y_l[b, at, :], y_r[b, at, :]], axis=1) for b in range(n_half)], axis=0
        )
        edges[...] = dot(outer, wide(w_edge))
        first_64 = iota((SUB, 128), 1) < B
        for h in range(2):
            lhs = jnp.concatenate([wide(mom, h * n_half + b, at) for b in range(n_half)], axis=0)
            total = dot(lhs, wide(w_own))
            edges_here = edges[:, 128 * h : 128 * h + 128]
            for b in range(0, n_half, 2):
                for u in range(CH):
                    place = half + h * half + b * SUB
                    tiles = ([], [])
                    for v in range(2):
                        piece = slice(((b + v) * CH + u) * SUB, ((b + v) * CH + u + 1) * SUB)
                        edge = edges_here[piece]
                        tiles[0].append(total[piece, :128] + jnp.where(first_64, edge, 0.0))
                        tiles[1].append(total[piece, 128:] + jnp.where(first_64, 0.0, edge))
                    for w in range(2):
                        both = jnp.concatenate(tiles[w], axis=0) * (1.0 / (B + 1))
                        rows_sm[w, c * CH + u, place : place + 2 * SUB, :] = both.astype(BF16)

        @pl.when(has_upper)
        def _():
            to_upper(c).start()

        @pl.when(has_lower)
        def _():
            to_lower(c).start()

    def smooth_columns(c):
        @pl.when(has_upper)
        def _():
            to_lower(c).wait_recv()

        @pl.when(has_lower)
        def _():
            to_upper(c).wait_recv()

        for u in range(0, CH, 2):
            k = c * CH + u
            pair = [dot(wide(w_col), wide(rows_sm, k + v)) * (1.0 / (B + 1) ** 2) for v in range(2)]
            sm[k] = pair[0].astype(BF16)
            sm[k + 1] = pair[1].astype(BF16)
            at = pl.ds(pl.multiple_of(k * SUB, 2 * SUB), 2 * SUB)
            for r in range(0, rows, 2 * SUB):
                store_wide(sm_b, r // SUB, at, pair[0][r : r + 2 * SUB], pair[1][r : r + 2 * SUB])

    pieces = channels // 8
    own_pieces = 2 * pieces // nx

    def send_all(number, peers, me, copy):
        def send(o, carry):
            copy(number, (me + o) % peers).start()
            return carry

        lax.fori_loop(1, peers, send, 0)

    def land_all(number, landed):
        pltpu.make_async_copy(landed, landed, ar_recv.at[number]).wait()
        pltpu.make_async_copy(landed, landed, ar_send.at[number]).wait()

    def own(g):
        return pl.ds(g * own_pieces, own_pieces)

    def remote(number, src, dst, device):
        return pltpu.make_async_remote_copy(
            src_ref=src,
            dst_ref=dst,
            send_sem=ar_send.at[number],
            recv_sem=ar_recv.at[number],
            device_id=device,
            device_id_type=MESH,
        )

    def scatter(number, g):
        return remote(number, part.at[own(g)], got1.at[gx], (g, gy))

    def across(number, g):
        return remote(number, sum1, got2.at[gy], (gx, g))

    def gather(number, g):
        return remote(number, sum2, got3.at[own(gx)], (g, gy))

    def tail_x(number, g):
        return remote(number, tile, got4.at[gx], (g, gy))

    def tail_y(number, g):
        return remote(number, sum4, got5.at[gy], (gx, g))

    def early_scatter():
        count = jnp.sum(jnp.sum(land_float[...], axis=0, keepdims=True), axis=1, keepdims=True)
        columns = jnp.sum(jnp.sum(sums[...].reshape(channels, SUB, cols), axis=1), axis=1, keepdims=True)
        right_half = iota((channels, 128), 1) >= channels
        as_row = jnp.sum(
            jnp.where(iota((channels, 128), 1) - channels == iota((channels, 128), 0), columns, 0.0),
            axis=0,
            keepdims=True,
        )
        part[0:pieces] = jnp.where(right_half, count, cov[...]).reshape(pieces, 8, 128)
        part[pieces : 2 * pieces] = jnp.where(right_half, as_row, jac[...]).reshape(pieces, 8, 128)
        got1[gx] = part[own(gx)]
        send_all(0, nx, gx, scatter)

    def early_across():
        land_all(0, got1.at[0 : nx - 1])
        sum1[...] = jnp.sum(got1[...], axis=0)
        got2[gy] = sum1[...]
        send_all(1, ny, gy, across)

    def early_gather():
        land_all(1, got2.at[0 : ny - 1])
        sum2[...] = jnp.sum(got2[...], axis=0)
        got3[own(gx)] = sum2[...]
        send_all(2, nx, gx, gather)

    last = n_chunks + LAG - 1

    def pipeline(t, carry):
        @pl.when(t < n_chunks)
        def _():
            smooth_rows(t)

        @pl.when(t == 0)
        def _():
            lax.fori_loop(0, channels // 2, block_regressors, 0)
            lax.fori_loop(0, channels * SUB // 64, moment_sums, 0)

        for g in range(channels // JAC_BLOCK):

            @pl.when(jnp.logical_or(t == 1 + 2 * g, t == 2 + 2 * g))
            def _(g=g):
                for u in range(0, blocks // 2, 2):
                    jac_part(g * JAC_BLOCK, (t - 1 - 2 * g) * (blocks // 2) + u)

            @pl.when(t == 2 + 2 * g)
            def _(g=g):
                jac_fold(g * JAC_BLOCK)

        first, count = COV_BLOCKS[0]
        begin = (first + count) // CH + LAG

        @pl.when(jnp.logical_or(t == begin, t == begin + 1))
        def _(first=first, count=count, begin=begin):
            for u in range(0, blocks // 2, 2):
                cov_part(first, count, (t - begin) * (blocks // 2) + u)

        @pl.when(t == begin + 1)
        def _(first=first, count=count):
            cov_fold(cov, first, count)
            early_scatter()

        first, count = COV_BLOCKS[1]
        begin = (first + count) // CH + LAG

        @pl.when(t == begin)
        def _(first=first, count=count):
            early_across()
            for b in range(0, blocks, 2):
                cov_part(first, count, b)
            cov_fold(cov_tail, first, count)

        @pl.when(t == last)
        def _():
            early_gather()

        @pl.when(t >= LAG)
        def _():
            smooth_columns(t - LAG)

        return carry

    lax.fori_loop(0, last + 1, pipeline, 0)

    first, count = COV_BLOCKS[2]
    for b in range(0, blocks, 2):
        cov_part(first, count, b)
    cov_fold(cov_tail, first, count)

    lane_group = iota((8, 128), 1) // 32
    packed = jnp.zeros((8, 128), F32)
    for g in range((channels - TAIL) // 8):
        piece = cov_tail[TAIL + 8 * g : TAIL + 8 * g + 8, :]
        packed = jnp.where(lane_group == g, pltpu.roll(piece, (32 * g - TAIL) % 128, 1), packed)
    tile[...] = packed
    send_all(3, nx, gx, tail_x)
    got4[gx] = tile[...]

    def drain(c, carry):
        @pl.when(has_left)
        def _():
            to_left(c).wait_send()

        @pl.when(has_right)
        def _():
            to_right(c).wait_send()

        @pl.when(has_upper)
        def _():
            to_upper(c).wait_send()

        @pl.when(has_lower)
        def _():
            to_lower(c).wait_send()

        return carry

    lax.fori_loop(0, n_chunks, drain, 0)
    land_all(2, got3.at[0 : (nx - 1) * own_pieces])
    total_v[...] = got3[...].reshape(2 * channels, 128)

    land_all(3, got4.at[0 : nx - 1])
    sum4[...] = jnp.sum(got4[...], axis=0)
    send_all(4, ny, gy, tail_y)
    got5[gy] = sum4[...]
    land_all(4, got5.at[0 : ny - 1])
    tail_v[...] = jnp.sum(got5[...], axis=0)


def finish(s_in, total_v, tail_v, coef_v, wgt_v, s_out, hac_v, new_v, sem):
    channels = s_in.shape[0]
    share = channels // 4

    def move(c):
        at = pl.ds(c * share, share)
        return pltpu.make_async_copy(s_in.at[at], s_out.at[at], sem.at[c])

    for c in range(4):
        move(c).start()
    first, second = total_v[0:channels, :], total_v[channels : 2 * channels, :]
    land_total = first[:, channels : channels + 1]
    tail = jnp.concatenate([pltpu.roll(tail_v[...], (TAIL - 32 * g) % 128, 1) for g in range((channels - TAIL) // 8)], axis=0)
    bottom = jnp.where(iota(tail.shape, 1) >= TAIL, tail, first[TAIL:, :])
    lower = jnp.concatenate([first[:TAIL, :], bottom], axis=0)[:, :channels]
    row, column = iota((channels, channels), 0), iota((channels, channels), 1)
    held = row >= 0
    for start, count in COV_BLOCKS:
        held = jnp.logical_and(held, jnp.logical_or(column < start, row >= start))
    hac_v[...] = jnp.where(held, lower, lower.T) * ((B + 1) / land_total)
    mean = second[0:1, channels:] / land_total[0:1, :]
    weighed = jnp.sum(wgt_v[...] * mean, axis=1, keepdims=True)
    jacobian = -second[:, :channels] / land_total
    gradient = 2.0 * jnp.sum(jacobian * weighed, axis=0, keepdims=True)
    new_v[...] = coef_v[...] - step_rate * gradient
    for c in range(4):
        move(c).wait()


def local(nx, ny, instruments, regressors, outcome, land_mask, coefficients, weighting):
    channels, rows, cols = instruments.shape
    n_chunks = channels // CH
    pieces = channels // 8
    own = 2 * pieces // nx
    blocks = rows // SUB
    any_spec = pl.BlockSpec(memory_space=pl.ANY)
    in_hbm = functools.partial(pltpu.with_memory_space_constraint, memory_space=pltpu.HBM)
    in_vmem = functools.partial(pltpu.with_memory_space_constraint, memory_space=pltpu.VMEM)
    hbm_spec = pl.BlockSpec(memory_space=pltpu.HBM)
    vmem_spec = pl.BlockSpec(memory_space=pltpu.VMEM)
    dma = pltpu.SemaphoreType.DMA
    blocked = pltpu.VMEM((2, blocks, channels * SUB, 128), BF16)
    edge = pltpu.VMEM((blocks // 2, channels * SUB, 128), BF16)
    smoothed, totals, tail = pl.pallas_call(
        functools.partial(kernel, nx, ny),
        out_shape=(
            pltpu.VMEM((channels, rows, cols), BF16),
            pltpu.VMEM((2 * channels, 128), F32),
            pltpu.VMEM((8, 128), F32),
        ),
        in_specs=[hbm_spec] * 5,
        out_specs=(vmem_spec, vmem_spec, vmem_spec),
        scratch_shapes=[
            pltpu.VMEM((channels, rows, cols), BF16),
            pltpu.VMEM((channels, rows, cols), BF16),
            pltpu.VMEM((rows, cols), F32),
            pltpu.VMEM((rows, cols), jnp.int32),
            pltpu.SMEM((channels,), F32),
            pltpu.VMEM((channels, SUB, 128), F32),
            pltpu.VMEM((rows, cols), F32),
            pltpu.VMEM((rows, cols), F32),
            blocked,
            blocked,
            blocked,
            edge,
            edge,
            edge,
            edge,
            pltpu.VMEM((2, channels, 2 * rows, 128), BF16),
            blocked,
            pltpu.VMEM((2, cols, 128), BF16),
            pltpu.VMEM((2, cols, 128), BF16),
            pltpu.VMEM((2, rows, 128), BF16),
            pltpu.VMEM((blocks // 2 * CH * SUB, cols), F32),
            pltpu.VMEM((channels * SUB, 32 * SUB), F32),
            pltpu.VMEM((channels * SUB, 32 * SUB), F32),
            pltpu.VMEM((channels, 128), F32),
            pltpu.VMEM((channels, 128), F32),
            pltpu.VMEM((channels, 128), F32),
            pltpu.VMEM((channels * SUB, cols), F32),
            pltpu.VMEM((2 * pieces, 8, 128), F32),
            pltpu.VMEM((nx, own, 8, 128), F32),
            pltpu.VMEM((own, 8, 128), F32),
            pltpu.VMEM((ny, own, 8, 128), F32),
            pltpu.VMEM((own, 8, 128), F32),
            pltpu.VMEM((2 * pieces, 8, 128), F32),
            pltpu.VMEM((8, 128), F32),
            pltpu.VMEM((nx, 8, 128), F32),
            pltpu.VMEM((8, 128), F32),
            pltpu.VMEM((ny, 8, 128), F32),
            dma((3,)),
            dma((4,)),
            dma((n_chunks,)),
        ]
        + [dma((n_chunks,))] * 8
        + [dma((5,)), dma((5,))],
        compiler_params=pltpu.CompilerParams(
            collective_id=0, has_side_effects=True, vmem_limit_bytes=42 * 1024 * 1024
        ),
        cost_estimate=pl.CostEstimate(flops=5 * 10**9, bytes_accessed=13 * 2**20, transcendentals=0),
    )(*map(in_hbm, (instruments, regressors, outcome, land_mask, coefficients)))
    smoothed, hac_cov, new_coefficients = pl.pallas_call(
        finish,
        out_shape=(
            jax.ShapeDtypeStruct((channels, rows, cols), BF16),
            jax.ShapeDtypeStruct((channels, channels), F32),
            jax.ShapeDtypeStruct((1, channels), F32),
        ),
        in_specs=[vmem_spec] * 5,
        out_specs=(any_spec, vmem_spec, vmem_spec),
        scratch_shapes=[dma((4,))],
        compiler_params=pltpu.CompilerParams(vmem_limit_bytes=4 * 1024 * 1024),
        cost_estimate=pl.CostEstimate(flops=10**6, bytes_accessed=8 * 2**20, transcendentals=0),
    )(in_vmem(smoothed), in_vmem(totals), in_vmem(tail), coefficients.reshape(1, channels), weighting)
    return smoothed, hac_cov, new_coefficients.reshape(channels)


def solution(mesh):
    placed = (P(None, "gx", "gy"), P(None, "gx", "gy"), P("gx", "gy"), P("gx", "gy"), P(), P())
    return jax.shard_map(
        functools.partial(local, mesh.shape["gx"], mesh.shape["gy"]),
        mesh=mesh,
        in_specs=placed,
        out_specs=(P(None, "gx", "gy"), P(), P()),
        check_vma=False,
    )
```

```python
import functools

import jax
import jax.numpy as jnp
from jax import lax
from jax.experimental import pallas as pl
from jax.experimental.pallas import tpu as pltpu
from jax.sharding import PartitionSpec as P

B = 64
step_rate = 0.05
MESH = pl.DeviceIdType.MESH
F32 = jnp.float32
BF16 = jnp.bfloat16
CH = 4
SUB = 8
LAG = 2
COV_BLOCKS = ((0, 32), (32, 16), (48, 16))
JAC_BLOCK = 32
TAIL = 32


def iota(shape, dim):
    return lax.broadcasted_iota(jnp.int32, shape, dim)


def dot(a, b):
    return lax.dot_general(a, b, (((1,), (0,)), ((), ())), preferred_element_type=F32)


def dot_t(a, b):
    return lax.dot_general(a, b, (((1,), (1,)), ((), ())), preferred_element_type=F32)


def wide(ref, *at):
    return jnp.concatenate([ref[(0, *at)], ref[(1, *at)]], axis=-1)


def put_wide(ref, value):
    ref[0] = value[:, :128]
    ref[1] = value[:, 128:]


def hat(distance):
    return jnp.maximum(B + 1 - jnp.abs(distance), 0).astype(F32).astype(BF16)


def kernel(
    nx,
    ny,
    inst_h,
    reg_h,
    outcome_h,
    land_h,
    coef_h,
    sm,
    total_v,
    tail_v,
    inst,
    reg,
    outcome,
    land,
    coef_s,
    coefs,
    weighted,
    land_float,
    mom,
    inst_b,
    reg_b,
    send_l,
    send_r,
    y_l,
    y_r,
    rows_sm,
    sm_b,
    w_own,
    w_edge,
    w_col,
    edges,
    acc_cov,
    acc_jac,
    cov,
    cov_tail,
    jac,
    sums,
    part,
    got1,
    sum1,
    got2,
    sum2,
    got3,
    tile,
    got4,
    sum4,
    got5,
    in_sem,
    reg_sem,
    inst_sem,
    yl_send,
    yl_recv,
    yr_send,
    yr_recv,
    zt_send,
    zt_recv,
    zb_send,
    zb_recv,
    ar_send,
    ar_recv,
):
    gx = lax.axis_index("gx")
    gy = lax.axis_index("gy")
    channels, rows, cols = inst.shape
    half = rows // 2
    n_chunks = channels // CH
    reg_rows = rows // 4
    blocks = rows // SUB

    def outcome_copy():
        return pltpu.make_async_copy(outcome_h, outcome, in_sem.at[0])

    def land_copy():
        return pltpu.make_async_copy(land_h, land, in_sem.at[1])

    def coef_copy():
        return pltpu.make_async_copy(coef_h, coef_s, in_sem.at[2])

    def reg_copy(r):
        at = pl.ds(pl.multiple_of(r * reg_rows, reg_rows), reg_rows)
        return pltpu.make_async_copy(reg_h.at[:, at, :], reg.at[:, at, :], reg_sem.at[r])

    def inst_copy(c):
        at = pl.ds(c * CH, CH)
        return pltpu.make_async_copy(inst_h.at[at], inst.at[at], inst_sem.at[c])

    coef_copy().start()
    reg_copy(0).start()
    outcome_copy().start()
    land_copy().start()
    for r in range(1, 4):
        reg_copy(r).start()
    for c in range(n_chunks):
        inst_copy(c).start()

    barrier = pltpu.get_barrier_semaphore()

    def greet_x(o, carry):
        pl.semaphore_signal(barrier, inc=1, device_id=((gx + o) % nx, gy), device_id_type=MESH)
        return carry

    def greet_y(o, carry):
        pl.semaphore_signal(barrier, inc=1, device_id=(gx, (gy + o) % ny), device_id_type=MESH)
        return carry

    lax.fori_loop(1, nx, greet_x, 0)
    lax.fori_loop(1, ny, greet_y, 0)

    src = iota((cols, cols), 0)
    dst = iota((cols, cols), 1)
    put_wide(w_own, hat(src - dst))
    lane = jnp.bitwise_and(dst, 127)
    column = jnp.where(lane < B, lane, lane + cols - 128)
    low = jnp.bitwise_and(src, B - 1)
    side = jnp.where(src < 2 * B, low - B, low + cols)
    same_half = (jnp.bitwise_and(src, B) == 0) == (dst < 128)
    put_wide(w_edge, jnp.where(same_half, jnp.maximum(B + 1 - jnp.abs(side - column), 0), 0).astype(F32).astype(BF16))
    put_wide(w_col, hat(iota((rows, 2 * rows), 1) - half - iota((rows, 2 * rows), 0)))

    @pl.when(gy == 0)
    def _():
        y_l[...] = jnp.zeros_like(y_l)

    @pl.when(gy == ny - 1)
    def _():
        y_r[...] = jnp.zeros_like(y_r)

    def clear(start):
        def body(k, carry):
            rows_sm[:, k, start : start + half, :] = jnp.zeros((2, half, 128), BF16)
            return carry

        lax.fori_loop(0, channels, body, 0)

    @pl.when(gx == 0)
    def _():
        clear(0)

    @pl.when(gx == nx - 1)
    def _():
        clear(rows + half)

    cov[...] = jnp.zeros_like(cov)
    cov_tail[...] = jnp.zeros_like(cov_tail)
    jac[...] = jnp.zeros_like(jac)
    acc_cov[...] = jnp.zeros_like(acc_cov)
    acc_jac[...] = jnp.zeros_like(acc_jac)

    coef_copy().wait()
    for p in range(channels):
        coefs[p] = jnp.full((SUB, 128), coef_s[p], F32)
    coefs[...] = coefs[...].astype(BF16).astype(F32)

    def residuals(r, carry):
        reg_copy(r).wait()
        at = pl.ds(pl.multiple_of(r * reg_rows, reg_rows), reg_rows)

        def add(q, total):
            for u in range(8):
                p = q * 8 + u
                one = jnp.concatenate([coefs[p]] * (cols // 128), axis=1)
                total = total + reg[p, at, :].astype(F32) * jnp.concatenate([one] * (reg_rows // SUB), axis=0)
            return total

        fitted = lax.fori_loop(0, channels // 8, add, jnp.zeros((reg_rows, cols), F32))

        @pl.when(r == 0)
        def _():
            outcome_copy().wait()
            land_copy().wait()

        here = land[at, :].astype(F32)
        weighted[at, :] = here * (outcome[at, :] - fitted)
        land_float[at, :] = here
        return carry

    lax.fori_loop(0, 4, residuals, 0)

    def chunk_rows(c):
        return pl.ds(pl.multiple_of(c * CH * SUB, CH * SUB), CH * SUB)

    def to_left(c):
        return pltpu.make_async_remote_copy(
            src_ref=send_l.at[:, chunk_rows(c), :],
            dst_ref=y_r.at[:, chunk_rows(c), :],
            send_sem=yl_send.at[c],
            recv_sem=yr_recv.at[c],
            device_id=(gx, gy - 1),
            device_id_type=MESH,
        )

    def to_right(c):
        return pltpu.make_async_remote_copy(
            src_ref=send_r.at[:, chunk_rows(c), :],
            dst_ref=y_l.at[:, chunk_rows(c), :],
            send_sem=yr_send.at[c],
            recv_sem=yl_recv.at[c],
            device_id=(gx, gy + 1),
            device_id_type=MESH,
        )

    def to_upper(c):
        at = pl.ds(c * CH, CH)
        return pltpu.make_async_remote_copy(
            src_ref=rows_sm.at[:, at, half : 2 * half, :],
            dst_ref=rows_sm.at[:, at, 3 * half : 4 * half, :],
            send_sem=zt_send.at[c],
            recv_sem=zb_recv.at[c],
            device_id=(gx - 1, gy),
            device_id_type=MESH,
        )

    def to_lower(c):
        at = pl.ds(c * CH, CH)
        return pltpu.make_async_remote_copy(
            src_ref=rows_sm.at[:, at, 2 * half : 3 * half, :],
            dst_ref=rows_sm.at[:, at, 0:half, :],
            send_sem=zb_send.at[c],
            recv_sem=zt_recv.at[c],
            device_id=(gx + 1, gy),
            device_id_type=MESH,
        )

    has_left, has_right = gy > 0, gy < ny - 1
    has_upper, has_lower = gx > 0, gx < nx - 1

    def send_edges(c):
        @pl.when(has_left)
        def _():
            to_left(c).start()

        @pl.when(has_right)
        def _():
            to_right(c).start()

    first_lanes = iota((2 * SUB, 128), 1) < B

    def store_blocked(ref, first_block, at, one, two):
        ref[first_block, at, :] = jnp.concatenate([one[:SUB], two[:SUB]], axis=0).astype(BF16)
        ref[first_block + 1, at, :] = jnp.concatenate([one[SUB:], two[SUB:]], axis=0).astype(BF16)

    def store_wide(ref, first_block, at, one, two):
        for h in range(2):
            lanes = slice(128 * h, 128 * h + 128)
            store_blocked(ref.at[h], first_block, at, one[:, lanes], two[:, lanes])

    def moments(c, carry):
        inst_copy(c).wait()

        def channel_pair(u, inner):
            k = c * CH + 2 * u
            at = pl.ds(pl.multiple_of(k * SUB, 2 * SUB), 2 * SUB)
            for r in range(0, half, 2 * SUB):
                first = r // SUB
                upper, lower = slice(r, r + 2 * SUB), slice(half + r, half + r + 2 * SUB)
                w_upper, w_lower = weighted[upper, :], weighted[lower, :]
                raw = [(inst[k + v, upper, :].astype(F32), inst[k + v, lower, :].astype(F32)) for v in range(2)]
                prods = [(top * w_upper, bot * w_lower) for top, bot in raw]
                store_wide(inst_b, first, at, raw[0][0], raw[1][0])
                store_wide(inst_b, blocks // 2 + first, at, raw[0][1], raw[1][1])
                store_wide(mom, first, at, prods[0][0], prods[1][0])
                store_wide(mom, blocks // 2 + first, at, prods[0][1], prods[1][1])
                left = [
                    jnp.where(first_lanes, top[:, :128], pltpu.roll(bot[:, :128], B, 1)) for top, bot in prods
                ]
                right = [
                    jnp.where(first_lanes, pltpu.roll(top[:, cols - 128 :], B, 1), bot[:, cols - 128 :])
                    for top, bot in prods
                ]
                store_blocked(send_l, first, at, left[0], left[1])
                store_blocked(send_r, first, at, right[0], right[1])
            return inner

        lax.fori_loop(0, CH // 2, channel_pair, 0)

        @pl.when(c == 0)
        def _():
            pl.semaphore_wait(barrier, nx - 1 + ny - 1)

        send_edges(c)
        return carry

    lax.fori_loop(0, n_chunks, moments, 0)

    def block_regressors(u, carry):
        at = pl.ds(pl.multiple_of(2 * u * SUB, 2 * SUB), 2 * SUB)
        for r in range(0, rows, 2 * SUB):
            here = land_float[r : r + 2 * SUB, :]
            one = reg[2 * u, r : r + 2 * SUB, :].astype(F32) * here
            two = reg[2 * u + 1, r : r + 2 * SUB, :].astype(F32) * here
            store_wide(reg_b, r // SUB, at, one, two)
        return carry

    def product(acc, left_ref, left_rows, right_ref, right_rows, b):
        at = (slice(0, left_rows.size), slice(0, right_rows.size))
        for u in range(2):
            acc[at] += dot_t(wide(left_ref, b + u, left_rows), wide(right_ref, b + u, right_rows))

    def fold(acc, left_count, right_count, first_column):
        at = (slice(0, left_count * SUB), slice(0, right_count * SUB))
        shape = (1, SUB, right_count * SUB)
        kept = jnp.where(jnp.bitwise_and(iota(shape, 2), SUB - 1) == iota(shape, 1), acc[at].reshape(left_count, SUB, right_count * SUB), 0.0)
        kept = jnp.sum(kept, axis=1)
        from_pick = iota((right_count * SUB, 128), 0) - (iota((right_count * SUB, 128), 1) - first_column) * SUB
        pick = jnp.logical_and(from_pick >= 0, from_pick < SUB)
        acc[...] = jnp.zeros_like(acc)
        return lax.dot_general(
            kept,
            pick.astype(F32),
            (((1,), (0,)), ((), ())),
            precision=lax.Precision.HIGHEST,
            preferred_element_type=F32,
        )

    def jac_part(first, b):
        at = pl.ds(pl.multiple_of(first * SUB, JAC_BLOCK * SUB), JAC_BLOCK * SUB)
        product(acc_jac, inst_b, pl.ds(0, channels * SUB), reg_b, at, b)

    def jac_fold(first):
        jac[...] += fold(acc_jac, channels, JAC_BLOCK, first)

    def cov_part(first, count, b):
        left = pl.ds(first * SUB, (channels - first) * SUB)
        product(acc_cov, mom, left, sm_b, pl.ds(first * SUB, count * SUB), b)

    def cov_fold(ref, first, count):
        ref[first:, :] += fold(acc_cov, channels - first, count, first)

    def moment_sums(q, carry):
        at = pl.ds(pl.multiple_of(q * 64, 64), 64)
        total = wide(mom, 0, at).astype(F32)
        for b in range(1, blocks):
            total = total + wide(mom, b, at).astype(F32)
        sums[at, :] = total
        return carry

    def smooth_rows(c):
        @pl.when(has_left)
        def _():
            to_right(c).wait_recv()

        @pl.when(has_right)
        def _():
            to_left(c).wait_recv()

        at = chunk_rows(c)
        n_half = half // SUB
        outer = jnp.concatenate(
            [jnp.concatenate([y_l[b, at, :], y_r[b, at, :]], axis=1) for b in range(n_half)], axis=0
        )
        edges[...] = dot(outer, wide(w_edge))
        first_64 = iota((SUB, 128), 1) < B
        for h in range(2):
            lhs = jnp.concatenate([wide(mom, h * n_half + b, at) for b in range(n_half)], axis=0)
            total = dot(lhs, wide(w_own))
            edges_here = edges[:, 128 * h : 128 * h + 128]
            for b in range(0, n_half, 2):
                for u in range(CH):
                    place = half + h * half + b * SUB
                    tiles = ([], [])
                    for v in range(2):
                        piece = slice(((b + v) * CH + u) * SUB, ((b + v) * CH + u + 1) * SUB)
                        edge = edges_here[piece]
                        tiles[0].append(total[piece, :128] + jnp.where(first_64, edge, 0.0))
                        tiles[1].append(total[piece, 128:] + jnp.where(first_64, 0.0, edge))
                    for w in range(2):
                        both = jnp.concatenate(tiles[w], axis=0) * (1.0 / (B + 1))
                        rows_sm[w, c * CH + u, place : place + 2 * SUB, :] = both.astype(BF16)

        @pl.when(has_upper)
        def _():
            to_upper(c).start()

        @pl.when(has_lower)
        def _():
            to_lower(c).start()

    def smooth_columns(c):
        @pl.when(has_upper)
        def _():
            to_lower(c).wait_recv()

        @pl.when(has_lower)
        def _():
            to_upper(c).wait_recv()

        for u in range(0, CH, 2):
            k = c * CH + u
            pair = [dot(wide(w_col), wide(rows_sm, k + v)) * (1.0 / (B + 1) ** 2) for v in range(2)]
            sm[k] = pair[0].astype(BF16)
            sm[k + 1] = pair[1].astype(BF16)
            at = pl.ds(pl.multiple_of(k * SUB, 2 * SUB), 2 * SUB)
            for r in range(0, rows, 2 * SUB):
                store_wide(sm_b, r // SUB, at, pair[0][r : r + 2 * SUB], pair[1][r : r + 2 * SUB])

    pieces = channels // 8
    own_pieces = 2 * pieces // nx

    def send_all(number, peers, me, copy):
        def send(o, carry):
            copy(number, (me + o) % peers).start()
            return carry

        lax.fori_loop(1, peers, send, 0)

    def land_all(number, landed):
        pltpu.make_async_copy(landed, landed, ar_recv.at[number]).wait()
        pltpu.make_async_copy(landed, landed, ar_send.at[number]).wait()

    def own(g):
        return pl.ds(g * own_pieces, own_pieces)

    def remote(number, src, dst, device):
        return pltpu.make_async_remote_copy(
            src_ref=src,
            dst_ref=dst,
            send_sem=ar_send.at[number],
            recv_sem=ar_recv.at[number],
            device_id=device,
            device_id_type=MESH,
        )

    def scatter(number, g):
        return remote(number, part.at[own(g)], got1.at[gx], (g, gy))

    def across(number, g):
        return remote(number, sum1, got2.at[gy], (gx, g))

    def gather(number, g):
        return remote(number, sum2, got3.at[own(gx)], (g, gy))

    def tail_x(number, g):
        return remote(number, tile, got4.at[gx], (g, gy))

    def tail_y(number, g):
        return remote(number, sum4, got5.at[gy], (gx, g))

    def early_scatter():
        count = jnp.sum(jnp.sum(land_float[...], axis=0, keepdims=True), axis=1, keepdims=True)
        columns = jnp.sum(jnp.sum(sums[...].reshape(channels, SUB, cols), axis=1), axis=1, keepdims=True)
        right_half = iota((channels, 128), 1) >= channels
        as_row = jnp.sum(
            jnp.where(iota((channels, 128), 1) - channels == iota((channels, 128), 0), columns, 0.0),
            axis=0,
            keepdims=True,
        )
        part[0:pieces] = jnp.where(right_half, count, cov[...]).reshape(pieces, 8, 128)
        part[pieces : 2 * pieces] = jnp.where(right_half, as_row, jac[...]).reshape(pieces, 8, 128)
        got1[gx] = part[own(gx)]
        send_all(0, nx, gx, scatter)

    def early_across():
        land_all(0, got1.at[0 : nx - 1])
        sum1[...] = jnp.sum(got1[...], axis=0)
        got2[gy] = sum1[...]
        send_all(1, ny, gy, across)

    def early_gather():
        land_all(1, got2.at[0 : ny - 1])
        sum2[...] = jnp.sum(got2[...], axis=0)
        got3[own(gx)] = sum2[...]
        send_all(2, nx, gx, gather)

    last = n_chunks + LAG - 1

    def pipeline(t, carry):
        @pl.when(t < n_chunks)
        def _():
            smooth_rows(t)

        @pl.when(t == 0)
        def _():
            lax.fori_loop(0, channels // 2, block_regressors, 0)
            lax.fori_loop(0, channels * SUB // 64, moment_sums, 0)

        for g in range(channels // JAC_BLOCK):

            @pl.when(jnp.logical_or(t == 1 + 2 * g, t == 2 + 2 * g))
            def _(g=g):
                for u in range(0, blocks // 2, 2):
                    jac_part(g * JAC_BLOCK, (t - 1 - 2 * g) * (blocks // 2) + u)

            @pl.when(t == 2 + 2 * g)
            def _(g=g):
                jac_fold(g * JAC_BLOCK)

        first, count = COV_BLOCKS[0]
        begin = (first + count) // CH + LAG

        @pl.when(jnp.logical_or(t == begin, t == begin + 1))
        def _(first=first, count=count, begin=begin):
            for u in range(0, blocks // 2, 2):
                cov_part(first, count, (t - begin) * (blocks // 2) + u)

        @pl.when(t == begin + 1)
        def _(first=first, count=count):
            cov_fold(cov, first, count)
            early_scatter()

        first, count = COV_BLOCKS[1]
        begin = (first + count) // CH + LAG

        @pl.when(t == begin)
        def _(first=first, count=count):
            early_across()
            for b in range(0, blocks, 2):
                cov_part(first, count, b)
            cov_fold(cov_tail, first, count)

        @pl.when(t == last)
        def _():
            early_gather()

        @pl.when(t >= LAG)
        def _():
            smooth_columns(t - LAG)

        return carry

    lax.fori_loop(0, last + 1, pipeline, 0)

    first, count = COV_BLOCKS[2]
    for b in range(0, blocks, 2):
        cov_part(first, count, b)
    cov_fold(cov_tail, first, count)

    lane_group = iota((8, 128), 1) // 32
    packed = jnp.zeros((8, 128), F32)
    for g in range((channels - TAIL) // 8):
        piece = cov_tail[TAIL + 8 * g : TAIL + 8 * g + 8, :]
        packed = jnp.where(lane_group == g, pltpu.roll(piece, (32 * g - TAIL) % 128, 1), packed)
    tile[...] = packed
    send_all(3, nx, gx, tail_x)
    got4[gx] = tile[...]

    def drain(c, carry):
        @pl.when(has_left)
        def _():
            to_left(c).wait_send()

        @pl.when(has_right)
        def _():
            to_right(c).wait_send()

        @pl.when(has_upper)
        def _():
            to_upper(c).wait_send()

        @pl.when(has_lower)
        def _():
            to_lower(c).wait_send()

        return carry

    lax.fori_loop(0, n_chunks, drain, 0)
    land_all(2, got3.at[0 : (nx - 1) * own_pieces])
    total_v[...] = got3[...].reshape(2 * channels, 128)

    land_all(3, got4.at[0 : nx - 1])
    sum4[...] = jnp.sum(got4[...], axis=0)
    send_all(4, ny, gy, tail_y)
    got5[gy] = sum4[...]
    land_all(4, got5.at[0 : ny - 1])
    tail_v[...] = jnp.sum(got5[...], axis=0)


def finish(s_in, total_v, tail_v, coef_v, wgt_v, s_out, hac_v, new_v, sem):
    channels = s_in.shape[0]
    share = channels // 4

    def move(c):
        at = pl.ds(c * share, share)
        return pltpu.make_async_copy(s_in.at[at], s_out.at[at], sem.at[c])

    for c in range(4):
        move(c).start()
    first, second = total_v[0:channels, :], total_v[channels : 2 * channels, :]
    land_total = first[:, channels : channels + 1]
    tail = jnp.concatenate([pltpu.roll(tail_v[...], (TAIL - 32 * g) % 128, 1) for g in range((channels - TAIL) // 8)], axis=0)
    bottom = jnp.where(iota(tail.shape, 1) >= TAIL, tail, first[TAIL:, :])
    lower = jnp.concatenate([first[:TAIL, :], bottom], axis=0)[:, :channels]
    row, column = iota((channels, channels), 0), iota((channels, channels), 1)
    held = row >= 0
    for start, count in COV_BLOCKS:
        held = jnp.logical_and(held, jnp.logical_or(column < start, row >= start))
    hac_v[...] = jnp.where(held, lower, lower.T) * ((B + 1) / land_total)
    mean = second[0:1, channels:] / land_total[0:1, :]
    weighed = jnp.sum(wgt_v[...] * mean, axis=1, keepdims=True)
    jacobian = -second[:, :channels] / land_total
    gradient = 2.0 * jnp.sum(jacobian * weighed, axis=0, keepdims=True)
    new_v[...] = coef_v[...] - step_rate * gradient
    for c in range(4):
        move(c).wait()


def local(nx, ny, instruments, regressors, outcome, land_mask, coefficients, weighting):
    channels, rows, cols = instruments.shape
    n_chunks = channels // CH
    pieces = channels // 8
    own = 2 * pieces // nx
    blocks = rows // SUB
    any_spec = pl.BlockSpec(memory_space=pl.ANY)
    in_hbm = functools.partial(pltpu.with_memory_space_constraint, memory_space=pltpu.HBM)
    in_vmem = functools.partial(pltpu.with_memory_space_constraint, memory_space=pltpu.VMEM)
    hbm_spec = pl.BlockSpec(memory_space=pltpu.HBM)
    vmem_spec = pl.BlockSpec(memory_space=pltpu.VMEM)
    dma = pltpu.SemaphoreType.DMA
    blocked = pltpu.VMEM((2, blocks, channels * SUB, 128), BF16)
    edge = pltpu.VMEM((blocks // 2, channels * SUB, 128), BF16)
    smoothed, totals, tail = pl.pallas_call(
        functools.partial(kernel, nx, ny),
        out_shape=(
            pltpu.VMEM((channels, rows, cols), BF16),
            pltpu.VMEM((2 * channels, 128), F32),
            pltpu.VMEM((8, 128), F32),
        ),
        in_specs=[hbm_spec] * 5,
        out_specs=(vmem_spec, vmem_spec, vmem_spec),
        scratch_shapes=[
            pltpu.VMEM((channels, rows, cols), BF16),
            pltpu.VMEM((channels, rows, cols), BF16),
            pltpu.VMEM((rows, cols), F32),
            pltpu.VMEM((rows, cols), jnp.int32),
            pltpu.SMEM((channels,), F32),
            pltpu.VMEM((channels, SUB, 128), F32),
            pltpu.VMEM((rows, cols), F32),
            pltpu.VMEM((rows, cols), F32),
            blocked,
            blocked,
            blocked,
            edge,
            edge,
            edge,
            edge,
            pltpu.VMEM((2, channels, 2 * rows, 128), BF16),
            blocked,
            pltpu.VMEM((2, cols, 128), BF16),
            pltpu.VMEM((2, cols, 128), BF16),
            pltpu.VMEM((2, rows, 128), BF16),
            pltpu.VMEM((blocks // 2 * CH * SUB, cols), F32),
            pltpu.VMEM((channels * SUB, 32 * SUB), F32),
            pltpu.VMEM((channels * SUB, 32 * SUB), F32),
            pltpu.VMEM((channels, 128), F32),
            pltpu.VMEM((channels, 128), F32),
            pltpu.VMEM((channels, 128), F32),
            pltpu.VMEM((channels * SUB, cols), F32),
            pltpu.VMEM((2 * pieces, 8, 128), F32),
            pltpu.VMEM((nx, own, 8, 128), F32),
            pltpu.VMEM((own, 8, 128), F32),
            pltpu.VMEM((ny, own, 8, 128), F32),
            pltpu.VMEM((own, 8, 128), F32),
            pltpu.VMEM((2 * pieces, 8, 128), F32),
            pltpu.VMEM((8, 128), F32),
            pltpu.VMEM((nx, 8, 128), F32),
            pltpu.VMEM((8, 128), F32),
            pltpu.VMEM((ny, 8, 128), F32),
            dma((3,)),
            dma((4,)),
            dma((n_chunks,)),
        ]
        + [dma((n_chunks,))] * 8
        + [dma((5,)), dma((5,))],
        compiler_params=pltpu.CompilerParams(
            collective_id=0, has_side_effects=True, vmem_limit_bytes=42 * 1024 * 1024
        ),
        cost_estimate=pl.CostEstimate(flops=5 * 10**9, bytes_accessed=13 * 2**20, transcendentals=0),
    )(*map(in_hbm, (instruments, regressors, outcome, land_mask, coefficients)))
    smoothed, hac_cov, new_coefficients = pl.pallas_call(
        finish,
        out_shape=(
            jax.ShapeDtypeStruct((channels, rows, cols), BF16),
            jax.ShapeDtypeStruct((channels, channels), F32),
            jax.ShapeDtypeStruct((1, channels), F32),
        ),
        in_specs=[vmem_spec] * 5,
        out_specs=(any_spec, vmem_spec, vmem_spec),
        scratch_shapes=[dma((4,))],
        compiler_params=pltpu.CompilerParams(vmem_limit_bytes=4 * 1024 * 1024),
        cost_estimate=pl.CostEstimate(flops=10**6, bytes_accessed=8 * 2**20, transcendentals=0),
    )(in_vmem(smoothed), in_vmem(totals), in_vmem(tail), coefficients.reshape(1, channels), weighting)
    return smoothed, hac_cov, new_coefficients.reshape(channels)


def solution(mesh):
    placed = (P(None, "gx", "gy"), P(None, "gx", "gy"), P("gx", "gy"), P("gx", "gy"), P(), P())
    return jax.shard_map(
        functools.partial(local, mesh.shape["gx"], mesh.shape["gy"]),
        mesh=mesh,
        in_specs=placed,
        out_specs=(P(None, "gx", "gy"), P(), P()),
        check_vma=False,
    )
```
